32 devices in a mesh: gx: 4 (over z), gy: 2 (over core), ma: 4 (over y, x).
Axes of the slice: x: 2, y: 2, z: 4, core: 2. Of those that a mesh axis runs over, the one named last changes fastest.
Arguments:
- ensemble: float32 [80, 2, 16, 256], P('ma', None, 'gx', 'gy'), may hold values from -6 to 6
- wind_field: float32 [2, 2, 16, 256], P(None, None, 'gx', 'gy'), may hold values from -0.45 to 0.45
- obs_value: float32 [4, 1024], replicated, may hold values from -6 to 6
- obs_var: float32 [4, 1024], replicated, may hold values from 2 to 20
- obs_region: int32 [4, 1024], replicated, may hold values from 0 to 7, as said below
- obs_cell: int32 [4, 1024], replicated, may hold values from 0 to 1023
- block_order: int32 [4], replicated, may hold values from 0 to 3, each once
- localization: float32 [4, 2, 4, 1024], P('gx', 'gy'), may hold values from 0 to 1
Outputs:
- analysis: float32 [80, 2, 16, 256], P('ma', None, 'gx', 'gy')
The draws below stay inside these ranges and needn't reach their ends.
Inputs may be any that keep to these rules, and one draw needn't show every extreme that they name: `obs_region`: region index = first-dimension region * 2 + second-dimension region.
All inputs are finite; a program needn't handle non-finite values.
Results may differ from the reference program's by a relative error of at most 0.0001.
Values sent between devices are 32-bit elements; how exact they have to be, the bound alone decides.
A program may use at most 64 MiB of HBM per device.

```python
import math
import jax
import jax.numpy as jnp
from jax import lax

MEMBERS = 80
LEV = 2
STEPS = 2
BLOCKS = 4
OBS = 1024
CX = 4
CY = 128
RX = 4
RY = 2
NX = 16
NY = 256
CELLS = 1024


def owner_regions(key):
    return jax.random.randint(jax.random.fold_in(key, 11), (BLOCKS, OBS), 0, RX * RY)


def draw_obs_region(key, part):
    return owner_regions(key)


def draw_localization(key, part):
    owners = owner_regions(key)
    owner_x = (owners // RY).astype(jnp.float32)
    owner_y = (owners % RY).astype(jnp.float32)
    region_x = jnp.arange(RX).astype(jnp.float32)[:, None, None, None]
    region_y = jnp.arange(RY).astype(jnp.float32)[None, :, None, None]
    gap_x = jnp.abs(region_x - owner_x[None, None])
    gap_x = jnp.minimum(gap_x, RX - gap_x)
    gap_y = jnp.abs(region_y - owner_y[None, None])
    gap_y = jnp.minimum(gap_y, RY - gap_y)
    radius = max(RX * 1.0, 1.5)
    ratio = (gap_x * gap_x + gap_y * gap_y) / (radius * radius)
    bump = jnp.maximum(1.0 - ratio, 0.0) ** 2
    factor = jax.random.uniform(jax.random.fold_in(key, 12), (RX, RY, BLOCKS, OBS), jnp.float32, 0.5, 1.0)
    return (bump * factor).astype(jnp.float32)


def plant(result, rng, low, top_value):
    longest = result.shape.index(max(result.shape))
    spots = []
    for shift in (0, 1):
        where = [jax.random.randint(jax.random.fold_in(rng, axis), (), 0, length) for axis, length in enumerate(result.shape)]
        where[longest] = (where[longest] + shift) % result.shape[longest]
        spots.append(tuple(where))
    return result.at[spots[0]].set(low).at[spots[1]].set(top_value)


def block_scale(key, shape, pieces, low, high):
    loudness, own = 1.0, jax.random.fold_in(key, 6)
    for dim, blocks in pieces:
        draws = jnp.exp(jax.random.uniform(jax.random.fold_in(own, dim), (blocks,), jnp.float32, low / len(pieces), high / len(pieces)))
        loudness = loudness * jnp.repeat(draws, shape[dim] // blocks).reshape([-1 if axis == dim else 1 for axis in range(len(shape))])
    return loudness


def scatter_about(stream_key, shape, spread, limit, cuts=(), dtype=jnp.bfloat16):
    values = spread * jax.random.normal(stream_key, shape, jnp.float32)
    if cuts:
        values = values * block_scale(stream_key, shape, cuts, -0.22, 0.18)
    return jnp.clip(values, -limit, limit).astype(dtype)


def setup_inputs(seed: int = 0) -> dict:
    seeds = jax.random.split(jax.random.key(seed), 9)
    return {
        "ensemble": scatter_about(seeds[0], (MEMBERS, LEV, NX, NY), 1.0, 6.0, ((0, 4), (2, 4), (3, 2)), jnp.float32),
        "wind_field": jnp.clip(jax.random.uniform(seeds[1], (2, LEV, NX, NY), jnp.float32, -0.45, 0.45) * block_scale(seeds[1], (2, LEV, NX, NY), ((2, 4), (3, 2)), -0.4, 0.0), -0.45, 0.45),
        "obs_value": scatter_about(seeds[2], (BLOCKS, OBS), 1.0, 6.0, (), jnp.float32),
        "obs_var": jnp.clip(jnp.exp(jax.random.uniform(seeds[3], (BLOCKS, OBS), jnp.float32, math.log(2.0), math.log(20.0))), 2.0, 20.0),
        "obs_region": draw_obs_region(jax.random.fold_in(seeds[8], 71), 0),
        "obs_cell": plant(jax.random.randint(seeds[5], (BLOCKS, OBS), 0, CELLS), jax.random.fold_in(seeds[5], 1), 0, CELLS - 1).astype(jnp.int32),
        "block_order": jax.random.permutation(seeds[6], BLOCKS).astype(jnp.int32),
        "localization": draw_localization(jax.random.fold_in(seeds[8], 71), 0),
    }


KAPPA = 0.025

def advect(tracer, wind_field):
    east_wind = wind_field[0][None]
    north_wind = wind_field[1][None]
    west_side = jnp.roll(tracer, 1, axis=2)
    east_side = jnp.roll(tracer, -1, axis=2)
    south_side = jnp.roll(tracer, 1, axis=3)
    north_side = jnp.roll(tracer, -1, axis=3)
    return tracer - jnp.maximum(east_wind, 0.0) * (tracer - west_side) - jnp.minimum(east_wind, 0.0) * (east_side - tracer) - jnp.maximum(north_wind, 0.0) * (tracer - south_side) - jnp.minimum(north_wind, 0.0) * (north_side - tracer) + KAPPA * (east_side + west_side + north_side + south_side - 4.0 * tracer)

def mixing_matrix(prior_obs, observed, error_var, taper):
    denom = MEMBERS - 1.0
    obs_mean = lax.optimization_barrier(jnp.mean(prior_obs, axis=0))
    anomaly = prior_obs - obs_mean
    variance = lax.optimization_barrier(jnp.sum(anomaly * anomaly, axis=0)) / denom
    total_var = variance + error_var
    innovation = observed - obs_mean
    shrink = 1.0 / (1.0 + jnp.sqrt(error_var / total_var))
    gain_mean = taper * innovation / (denom * total_var)
    gain_spread = taper * shrink / (denom * total_var)
    shift_terms = jnp.dot(anomaly, gain_mean, precision=lax.Precision.HIGHEST)
    weighted = anomaly * gain_spread
    return shift_terms[:, None] - jnp.dot(weighted, anomaly.T, precision=lax.Precision.HIGHEST)

def reference(ensemble, wind_field, obs_value, obs_var, obs_region, obs_cell, block_order, localization):
    state = ensemble
    for step_index in range(STEPS):
        state = advect(state, wind_field)
    per_region = jax.vmap(jax.vmap(mixing_matrix, (None, None, None, 0)), (None, None, None, 0))
    for position in range(BLOCKS):
        block_id = block_order[position]
        regions = obs_region[block_id]
        cell_index = obs_cell[block_id]
        level_index = cell_index // (CX * CY)
        x_index = cell_index // CY % CX + regions // RY * CX
        y_index = cell_index % CY + regions % RY * CY
        prior_obs = state[:, level_index, x_index, y_index]
        taper = lax.dynamic_index_in_dim(localization, block_id, 2, keepdims=False)
        mixing = per_region(prior_obs, obs_value[block_id], obs_var[block_id], taper)
        center = lax.optimization_barrier(jnp.mean(state, axis=0))
        deviation = (state - center).reshape(MEMBERS, LEV, RX, CX, RY, CY)
        update = jnp.einsum('abpm,plaxby->mlaxby', mixing, deviation, precision=lax.Precision.HIGHEST)
        state = state + update.reshape(state.shape)
    return state
```

```python
import functools

import jax
import jax.numpy as jnp
from jax import lax
from jax.experimental import pallas as pl
from jax.experimental.pallas import tpu as pltpu
from jax.sharding import PartitionSpec as P

STEPS = 2
KAPPA = 0.025
PAD = 128
MESH = pl.DeviceIdType.MESH
BF = jnp.bfloat16
F32 = jnp.float32


def split(x):
    high = x.astype(BF)
    return high, (x - high.astype(F32)).astype(BF)


def kernel(
    nx, ny, nm,
    order_ref, ens_ref, wind_ref, value_ref, var_ref, region_ref, cell_ref, loc_ref,
    out_ref,
    o_ens, o_wind, up_ref, down_ref, low_ref, high_ref, ext_ref, piece_ref,
    all_ref, split_ref, loc_all, hot_ref, prior_ref, lhs_ref, gm_ref, anom_ref,
    send_ref, pair_ref, line_ref, full_ref,
    pre_sem, halo_sem, loc_send, loc_recv, plane_send, plane_recv,
    pair_sem, line_send, line_recv,
):
    members_dev, levels, cx, cy = ens_ref.shape
    half = members_dev // 2
    members = members_dev * nm
    blocks, obs = value_ref.shape
    cells = levels * cx * cy
    gx, gy, ma = lax.axis_index("gx"), lax.axis_index("gy"), lax.axis_index("ma")
    other = 1 - gy

    def remote(src, dst, send_sem, recv_sem, device):
        return pltpu.make_async_remote_copy(
            src_ref=src, dst_ref=dst, send_sem=send_sem, recv_sem=recv_sem,
            device_id=device, device_id_type=MESH,
        )

    line = [(lax.rem(gx + d, nx), c) for d in range(nx) for c in range(ny) if d or c]
    line = [(x, lax.rem(gy + c, ny)) for x, c in line]
    plane = [(lax.rem(ma + d, nm), lax.rem(gy + c, ny)) for d in range(nm) for c in range(ny) if d or c]

    barrier = pltpu.get_barrier_semaphore()
    for x, c in line:
        pl.semaphore_signal(barrier, inc=1, device_id=(x, c, ma), device_id_type=MESH)
    for m, c in plane[ny - 1:]:
        pl.semaphore_signal(barrier, inc=1, device_id=(gx, c, m), device_id_type=MESH)
    pl.semaphore_wait(barrier, len(line) + len(plane) - (ny - 1))

    swap = [
        remote(ens_ref.at[pl.ds(other * half, half)], o_ens, pre_sem.at[0], pre_sem.at[1], (gx, other, ma)),
        remote(wind_ref, o_wind, pre_sem.at[2], pre_sem.at[3], (gx, other, ma)),
    ]
    for copy in swap:
        copy.start()

    split_ref[...] = jnp.zeros_like(split_ref)
    anom_ref[...] = jnp.zeros_like(anom_ref)
    prior_ref[...] = jnp.zeros_like(prior_ref)

    for copy in swap:
        copy.wait()

    left = gy == 0
    own_t = ens_ref[pl.ds(gy * half, half)]
    for lev in range(levels):
        pairs = (
            (own_t[:, lev], o_ens[:, lev], slice(0, half)),
            (wind_ref[:, lev], o_wind[:, lev], slice(half, half + 2)),
        )
        for mine, theirs, where in pairs:
            first = jnp.where(left, mine, theirs)
            second = jnp.where(left, theirs, mine)
            for part, lanes in ((first, slice(0, cy)), (second, slice(cy, 2 * cy))):
                ext_ref[where, lev, 2:2 + cx, lanes] = part
                up_ref[where, 2 * lev:2 * lev + 2, lanes] = part[:, cx - 2:cx]
                down_ref[where, 2 * lev:2 * lev + 2, lanes] = part[:, 0:2]
    after, before = lax.rem(gx + 1, nx), lax.rem(gx + nx - 1, nx)
    halo = [
        remote(up_ref, low_ref, halo_sem.at[0], halo_sem.at[1], (after, gy, ma)),
        remote(down_ref, high_ref, halo_sem.at[2], halo_sem.at[3], (before, gy, ma)),
    ]
    for copy in halo:
        copy.start()

    own_region = gx * ny + gy
    loc_copies = []
    for i, (x, c) in enumerate(line):
        source = x * ny + c
        copy = remote(loc_ref.at[0, 0], loc_all.at[own_region], loc_send.at[i], loc_recv.at[own_region], (x, c, ma))
        copy.start()
        loc_copies.append((copy, remote(loc_ref.at[0, 0], loc_all.at[source], loc_send.at[i], loc_recv.at[source], (x, c, ma))))
    loc_all[own_region] = loc_ref[0, 0]

    def make_hot(k):
        b = order_ref[k]
        cell = jnp.where(region_ref[pl.ds(b, 1), :] == own_region, cell_ref[pl.ds(b, 1), :], -1)
        for s in range(cells // PAD):
            index = lax.broadcasted_iota(jnp.int32, (PAD, obs), 0) + s * PAD
            hot_ref[s * PAD:(s + 1) * PAD, :] = jnp.where(index == cell, 1.0, 0.0).astype(BF)

    make_hot(0)
    for copy in halo:
        copy.wait()

    for lev in range(levels):
        ext_ref[:, lev, 0:2, :] = low_ref[:, 2 * lev:2 * lev + 2, :]
        ext_ref[:, lev, 2 + cx:4 + cx, :] = high_ref[:, 2 * lev:2 * lev + 2, :]
    for lev in range(levels):
        east_wind = ext_ref[half, lev][None]
        north_wind = ext_ref[half + 1, lev][None]
        q = ext_ref[0:half, lev]
        for _ in range(STEPS):
            west = pltpu.roll(q, 1, 1)
            east = pltpu.roll(q, cx + 3, 1)
            south = pltpu.roll(q, 1, 2)
            north = pltpu.roll(q, 2 * cy - 1, 2)
            q = (
                q
                - jnp.maximum(east_wind, 0.0) * (q - west)
                - jnp.minimum(east_wind, 0.0) * (east - q)
                - jnp.maximum(north_wind, 0.0) * (q - south)
                - jnp.minimum(north_wind, 0.0) * (north - q)
                + KAPPA * (east + west + north + south - 4.0 * q)
            )
        for c in range(ny):
            piece_ref[c, :, lev * cx:(lev + 1) * cx, :] = q[:, 2:2 + cx, c * cy:(c + 1) * cy]

    own_part = ma * ny + gy
    plane_copies = []
    for i, (m, c) in enumerate(plane):
        source = m * ny + c
        copy = remote(
            piece_ref.at[c], all_ref.at[pl.ds(own_part * half, half)],
            plane_send.at[i], plane_recv.at[own_part], (gx, c, m),
        )
        copy.start()
        plane_copies.append((copy, remote(
            piece_ref.at[gy], all_ref.at[pl.ds(source * half, half)],
            plane_send.at[i], plane_recv.at[source], (gx, c, m),
        )))
    all_ref[pl.ds(own_part * half, half)] = piece_ref[gy]
    for sent, received in plane_copies:
        sent.wait_send()
        received.wait_recv()

    rows = levels * cx
    for s in range(rows):
        high, low = split(all_ref[:, s, :])
        split_ref[0, 0:members, s * cy:(s + 1) * cy] = high
        split_ref[1, 0:members, s * cy:(s + 1) * cy] = low

    def pick():
        for part in range(2):
            prior_ref[part, 0:members, :] = jnp.dot(
                split_ref[part, 0:members, :], hot_ref[...], preferred_element_type=F32
            ).astype(BF)

    pick()
    for sent, received in loc_copies:
        sent.wait_send()
        received.wait_recv()

    def apply(change, high, low):
        c_high, c_low = split(change)
        both = jnp.dot(jnp.concatenate([c_high, c_low], axis=0), high, preferred_element_type=F32)
        rest = jnp.dot(c_high, low, preferred_element_type=F32)
        return both[:members] + both[members:] + rest

    width = 4 if nx % 4 == 0 else nx
    in_group = width * ny
    lane = lax.broadcasted_iota(jnp.int32, (members, PAD), 1)
    change = None
    denom = members - 1.0
    for k in range(blocks):
        slot = k % 2
        b = order_ref[k]
        prior = prior_ref[0, 0:members, :].astype(F32) + prior_ref[1, 0:members, :].astype(F32)
        if k:
            prior = prior + apply(change, prior_ref[0], prior_ref[1])
        error_var = var_ref[pl.ds(b, 1), :]
        obs_mean = jnp.sum(prior, axis=0, keepdims=True) / members
        anomaly = prior - obs_mean
        variance = jnp.sum(anomaly * anomaly, axis=0, keepdims=True) / denom
        total_var = variance + error_var
        innovation = value_ref[pl.ds(b, 1), :] - obs_mean
        shrink = 1.0 / (1.0 + jnp.sqrt(error_var / total_var))
        scaled = 1.0 / (denom * total_var)
        mean_gain = innovation * scaled
        spread_gain = shrink * scaled
        a_high, a_low = split(anomaly)
        anom_ref[0:members, :] = a_high
        anom_ref[PAD:PAD + members, :] = a_low

        def group(g):
            for j in range(width):
                for c in range(ny):
                    i = j * ny + c
                    taper = loc_all[(g * width + j) * ny + c, pl.ds(b, 1), :]
                    w_high, w_low = split(anomaly * (taper * spread_gain))
                    lhs_ref[2 * i * members:(2 * i + 1) * members, :] = w_high
                    lhs_ref[(2 * i + 1) * members:(2 * i + 2) * members, :] = w_low
                    gm_ref[i:i + 1, :] = taper * mean_gain
            end = 2 * in_group * members
            g_high, g_low = split(gm_ref[...])
            lhs_ref[end:end + 16, :] = jnp.concatenate([g_high, g_low], axis=0)
            product = lax.dot_general(
                lhs_ref[...], anom_ref[...], (((1,), (1,)), ((), ())), preferred_element_type=F32
            )
            shift = product[end:end + 8, :PAD] + product[end:end + 8, PAD:] + product[end + 8:end + 16, :PAD]
            for j in range(width):
                for c in range(ny):
                    i = j * ny + c
                    first = product[2 * i * members:(2 * i + 1) * members]
                    second = product[(2 * i + 1) * members:(2 * i + 2) * members, :PAD]
                    spread = first[:, :PAD] + first[:, PAD:] + second
                    send_ref[slot, c, g * width + j] = shift[i:i + 1] - spread

        if nx == width:
            group(0)
        else:
            lax.fori_loop(0, nx // width, lambda g, carry: (group(g), carry)[1], 0)

        pair = remote(
            send_ref.at[slot, other], pair_ref.at[slot], pair_sem.at[slot, 0], pair_sem.at[slot, 1], (gx, other, ma)
        )
        pair.start()
        pair.wait()
        copies = []
        for d in range(nx):
            x = lax.rem(gx + d, nx)
            send_ref[slot, gy, x] = send_ref[slot, gy, x] + pair_ref[slot, x]
            if d:
                copy = remote(
                    send_ref.at[slot, gy, x], line_ref.at[slot, gx],
                    line_send.at[slot, d], line_recv.at[slot, gx], (x, gy, ma),
                )
                copy.start()
                copies.append((copy, remote(
                    send_ref.at[slot, gy, x], line_ref.at[slot, x],
                    line_send.at[slot, d], line_recv.at[slot, x], (x, gy, ma),
                )))
            else:
                line_ref[slot, gx] = send_ref[slot, gy, x]
        if k + 1 < blocks:
            make_hot(k + 1)
            pick()
        for sent, received in copies:
            sent.wait_send()
            received.wait_recv()
        mixing = line_ref[slot, 0]
        for x in range(1, nx):
            mixing = mixing + line_ref[slot, x]
        centre = jnp.sum(mixing, axis=1, keepdims=True) / members
        mixing = jnp.where(lane < members, mixing - centre, 0.0)
        if k:
            padded = jnp.concatenate([change, jnp.zeros((PAD - members, PAD), F32)], axis=0)
            change = change + mixing + jnp.dot(
                mixing, padded, precision=lax.Precision.HIGHEST, preferred_element_type=F32
            )
        else:
            change = mixing

    update = apply(change, split_ref[0], split_ref[1])
    for s in range(rows):
        full_ref[:, s, :] = all_ref[:, s, :] + update[:, s * cy:(s + 1) * cy]
    mine = full_ref[pl.ds(ma * members_dev, members_dev)]
    for lev in range(levels):
        out_ref[:, lev] = mine[:, lev * cx:(lev + 1) * cx, :]


def local(
    ensemble, wind_field, obs_value, obs_var, obs_region, obs_cell, block_order, localization
):
    nx, ny, nm = lax.axis_size("gx"), lax.axis_size("gy"), lax.axis_size("ma")
    members_dev, levels, cx, cy = ensemble.shape
    half = members_dev // 2
    members = members_dev * nm
    blocks, obs = obs_value.shape
    rows = levels * cx
    cells = rows * cy
    regions = nx * ny
    width = 4 if nx % 4 == 0 else nx
    in_group = width * ny
    dma = pltpu.SemaphoreType.DMA
    vmem = pl.BlockSpec(memory_space=pltpu.VMEM)
    return pl.pallas_call(
        functools.partial(kernel, nx, ny, nm),
        out_shape=jax.ShapeDtypeStruct(ensemble.shape, F32),
        in_specs=[pl.BlockSpec(memory_space=pltpu.SMEM)] + [vmem] * 7,
        out_specs=vmem,
        scratch_shapes=[
            pltpu.VMEM((half, levels, cx, cy), F32),
            pltpu.VMEM(wind_field.shape, F32),
            pltpu.VMEM((half + 2, 2 * levels, 2 * cy), F32),
            pltpu.VMEM((half + 2, 2 * levels, 2 * cy), F32),
            pltpu.VMEM((half + 2, 2 * levels, 2 * cy), F32),
            pltpu.VMEM((half + 2, 2 * levels, 2 * cy), F32),
            pltpu.VMEM((half + 2, levels, cx + 4, 2 * cy), F32),
            pltpu.VMEM((ny, half, rows, cy), F32),
            pltpu.VMEM((members, rows, cy), F32),
            pltpu.VMEM((2, PAD, cells), BF),
            pltpu.VMEM((regions, blocks, obs), F32),
            pltpu.VMEM((cells, obs), BF),
            pltpu.VMEM((2, PAD, obs), BF),
            pltpu.VMEM((2 * in_group * members + 16, obs), BF),
            pltpu.VMEM((8, obs), F32),
            pltpu.VMEM((2 * PAD, obs), BF),
            pltpu.VMEM((2, ny, nx, members, PAD), F32),
            pltpu.VMEM((2, nx, members, PAD), F32),
            pltpu.VMEM((2, nx, members, PAD), F32),
            pltpu.VMEM((members, rows, cy), F32),
            dma((4,)),
            dma((4,)),
            dma((regions,)),
            dma((regions,)),
            dma((nm * ny,)),
            dma((nm * ny,)),
            dma((2, 2)),
            dma((2, nx)),
            dma((2, nx)),
        ],
        compiler_params=pltpu.CompilerParams(
            collective_id=0, has_side_effects=True, vmem_limit_bytes=56 * 1024 * 1024
        ),
    )(block_order, ensemble, wind_field, obs_value, obs_var, obs_region, obs_cell, localization)


def solution(mesh):
    in_specs = (
        P("ma", None, "gx", "gy"),
        P(None, None, "gx", "gy"),
        P(),
        P(),
        P(),
        P(),
        P(),
        P("gx", "gy", None, None),
    )
    out_specs = P("ma", None, "gx", "gy")
    return jax.shard_map(local, mesh=mesh, in_specs=in_specs, out_specs=out_specs, check_vma=False)
```

```python
import functools

import jax
import jax.numpy as jnp
from jax import lax
from jax.experimental import pallas as pl
from jax.experimental.pallas import tpu as pltpu
from jax.sharding import PartitionSpec as P

STEPS = 2
KAPPA = 0.025
PAD = 128
MESH = pl.DeviceIdType.MESH
BF = jnp.bfloat16
F32 = jnp.float32


def split(x):
    high = x.astype(BF)
    return high, (x - high.astype(F32)).astype(BF)


def kernel(
    nx, ny, nm,
    order_ref, ens_ref, wind_ref, value_ref, var_ref, region_ref, cell_ref, loc_ref,
    out_ref,
    o_ens, o_wind, up_ref, down_ref, low_ref, high_ref, ext_ref, piece_ref,
    all_ref, flat_ref, split_ref, loc_all, hot_ref, lhs_ref, gm_ref, anom_ref,
    send_ref, pair_ref, line_ref,
    swap_sem, halo_send, halo_recv, loc_send, loc_recv, plane_send, plane_recv,
    pair_sem, line_send, line_recv,
):
    members_dev, levels, cx, cy = ens_ref.shape
    half = members_dev // 2
    members = members_dev * nm
    mid = members // 2
    blocks, obs = value_ref.shape
    cells = levels * cx * cy
    rows = levels * cx
    gx, gy, ma = lax.axis_index("gx"), lax.axis_index("gy"), lax.axis_index("ma")
    other = 1 - gy

    def remote(src, dst, send_sem, recv_sem, device):
        return pltpu.make_async_remote_copy(
            src_ref=src, dst_ref=dst, send_sem=send_sem, recv_sem=recv_sem,
            device_id=device, device_id_type=MESH,
        )

    line = [(lax.rem(gx + d, nx), c) for d in range(nx) for c in range(ny) if d or c]
    line = [(x, lax.rem(gy + c, ny)) for x, c in line]
    plane = [(lax.rem(ma + d, nm), lax.rem(gy + c, ny)) for d in range(nm) for c in range(ny) if d or c]

    barrier = pltpu.get_barrier_semaphore()
    for x, c in line:
        pl.semaphore_signal(barrier, inc=1, device_id=(x, c, ma), device_id_type=MESH)
    for m, c in plane[ny - 1:]:
        pl.semaphore_signal(barrier, inc=1, device_id=(gx, c, m), device_id_type=MESH)

    for c in range(ny):
        for lev in range(levels):
            pair_rows = slice(2 * lev, 2 * lev + 2)
            part = ens_ref[c * half:(c + 1) * half, lev]
            winds = wind_ref[:, lev]
            up_ref[c, 0:half, pair_rows, :] = part[:, cx - 2:cx]
            up_ref[c, half:half + 2, pair_rows, :] = winds[:, cx - 2:cx]
            down_ref[c, 0:half, pair_rows, :] = part[:, 0:2]
            down_ref[c, half:half + 2, pair_rows, :] = winds[:, 0:2]
    anom_ref[...] = jnp.zeros_like(anom_ref)
    gm_ref[...] = jnp.zeros_like(gm_ref)

    pl.semaphore_wait(barrier, len(line) + len(plane) - (ny - 1))

    after, before = lax.rem(gx + 1, nx), lax.rem(gx + nx - 1, nx)
    halo = []
    for c in range(ny):
        for way, (src, dst, to, source) in enumerate(
            ((up_ref, low_ref, after, before), (down_ref, high_ref, before, after))
        ):
            copy = remote(src.at[c], dst.at[gy], halo_send.at[way, c], halo_recv.at[way, gy], (to, c, ma))
            copy.start()
            halo.append((copy, remote(
                src.at[c], dst.at[c], halo_send.at[way, c], halo_recv.at[way, c], (source, c, ma)
            )))
    swap = [
        remote(ens_ref.at[pl.ds(other * half, half)], o_ens, swap_sem.at[0], swap_sem.at[1], (gx, other, ma)),
        remote(wind_ref, o_wind, swap_sem.at[2], swap_sem.at[3], (gx, other, ma)),
    ]
    for copy in swap:
        copy.start()

    own_region = gx * ny + gy
    loc_copies = []
    for i, (x, c) in enumerate(line):
        source = x * ny + c
        copy = remote(loc_ref.at[0, 0], loc_all.at[own_region], loc_send.at[i], loc_recv.at[own_region], (x, c, ma))
        copy.start()
        loc_copies.append((copy, remote(loc_ref.at[0, 0], loc_all.at[source], loc_send.at[i], loc_recv.at[source], (x, c, ma))))
    loc_all[own_region] = loc_ref[0, 0]

    def make_hot(k):
        b = order_ref[k]
        cell = jnp.where(region_ref[pl.ds(b, 1), :] == own_region, cell_ref[pl.ds(b, 1), :], -1)
        for s in range(cells // PAD):
            index = lax.broadcasted_iota(jnp.int32, (PAD, obs), 0) + s * PAD
            hot_ref[s * PAD:(s + 1) * PAD, :] = jnp.where(index == cell, 1.0, 0.0).astype(BF)

    make_hot(0)
    for copy in swap:
        copy.wait()

    left = gy == 0
    own_t = ens_ref[pl.ds(gy * half, half)]
    for lev in range(levels):
        pairs = (
            (own_t[:, lev], o_ens[:, lev], slice(0, half)),
            (wind_ref[:, lev], o_wind[:, lev], slice(half, half + 2)),
        )
        for mine, theirs, where in pairs:
            ext_ref[where, lev, 2:2 + cx, 0:cy] = jnp.where(left, mine, theirs)
            ext_ref[where, lev, 2:2 + cx, cy:2 * cy] = jnp.where(left, theirs, mine)
    for sent, received in halo:
        sent.wait_send()
        received.wait_recv()

    for lev in range(levels):
        for c in range(ny):
            lanes = slice(c * cy, (c + 1) * cy)
            ext_ref[:, lev, 0:2, lanes] = low_ref[c, :, 2 * lev:2 * lev + 2, :]
            ext_ref[:, lev, 2 + cx:4 + cx, lanes] = high_ref[c, :, 2 * lev:2 * lev + 2, :]
    for lev in range(levels):
        east_wind = ext_ref[half, lev][None]
        north_wind = ext_ref[half + 1, lev][None]
        q = ext_ref[0:half, lev]
        for _ in range(STEPS):
            west = pltpu.roll(q, 1, 1)
            east = pltpu.roll(q, cx + 3, 1)
            south = pltpu.roll(q, 1, 2)
            north = pltpu.roll(q, 2 * cy - 1, 2)
            q = (
                q
                - jnp.maximum(east_wind, 0.0) * (q - west)
                - jnp.minimum(east_wind, 0.0) * (east - q)
                - jnp.maximum(north_wind, 0.0) * (q - south)
                - jnp.minimum(north_wind, 0.0) * (north - q)
                + KAPPA * (east + west + north + south - 4.0 * q)
            )
        for c in range(ny):
            piece_ref[c, :, lev * cx:(lev + 1) * cx, :] = q[:, 2:2 + cx, c * cy:(c + 1) * cy]

    own_part = ma * ny + gy
    plane_copies = []
    for i, (m, c) in enumerate(plane):
        source = m * ny + c
        copy = remote(
            piece_ref.at[c], all_ref.at[pl.ds(own_part * half, half)],
            plane_send.at[i], plane_recv.at[own_part], (gx, c, m),
        )
        copy.start()
        plane_copies.append((copy, remote(
            piece_ref.at[gy], all_ref.at[pl.ds(source * half, half)],
            plane_send.at[i], plane_recv.at[source], (gx, c, m),
        )))
    all_ref[pl.ds(own_part * half, half)] = piece_ref[gy]
    for sent, received in plane_copies:
        sent.wait_send()
        received.wait_recv()

    for s in range(rows):
        lanes = slice(s * cy, (s + 1) * cy)
        values = all_ref[:, s, :]
        flat_ref[:, lanes] = values
        high, low = split(values)
        split_ref[0:members, lanes] = high
        split_ref[members:2 * members, lanes] = low

    def pick():
        both = jnp.dot(split_ref[...], hot_ref[...], preferred_element_type=F32)
        return both[:members] + both[members:], both[:members].astype(BF), both[members:].astype(BF)

    def apply(change, high, low):
        c_high, c_low = split(change)
        c_high, c_low = c_high[:, :members], c_low[:, :members]
        both = jnp.dot(jnp.concatenate([c_high, c_low], axis=0), high, preferred_element_type=F32)
        rest = jnp.dot(c_high, low, preferred_element_type=F32)
        return both[:change.shape[0]] + both[change.shape[0]:] + rest

    def own_rows(x):
        own = x[0:members_dev]
        for m in range(1, nm):
            own = jnp.where(ma == m, x[m * members_dev:(m + 1) * members_dev], own)
        filler = jnp.zeros((-members_dev % 16, x.shape[1]), F32)
        return jnp.concatenate([own, filler], axis=0)

    width = 4 if nx % 4 == 0 else nx
    lane = lax.broadcasted_iota(jnp.int32, (members, PAD), 1)
    top_lane = lane[:mid]
    denom = members - 1.0
    prior = pick()[0]
    for sent, received in loc_copies:
        sent.wait_send()
        received.wait_recv()

    change = mixing = None
    for k in range(blocks):
        slot = k % 2
        b = order_ref[k]
        error_var = var_ref[pl.ds(b, 1), :]
        obs_mean = jnp.sum(prior, axis=0, keepdims=True) / members
        anomaly = prior - obs_mean
        variance = jnp.sum(anomaly * anomaly, axis=0, keepdims=True) / denom
        total_var = variance + error_var
        innovation = value_ref[pl.ds(b, 1), :] - obs_mean
        shrink = 1.0 / (1.0 + jnp.sqrt(error_var / total_var))
        scaled = 1.0 / (denom * total_var)
        mean_gain = innovation * scaled
        spread_gain = shrink * scaled
        a_high, a_low = split(anomaly)
        anom_ref[0:members, :] = a_high
        anom_ref[PAD:PAD + members, :] = a_low

        def group(c, turn, g):
            for j in range(width):
                taper = loc_all[(g * width + j) * ny + c, pl.ds(b, 1), :]
                w_high, w_low = split(anomaly * (taper * spread_gain))
                lhs_ref[turn, 2 * j * members:(2 * j + 1) * members, :] = w_high
                lhs_ref[turn, (2 * j + 1) * members:(2 * j + 2) * members, :] = w_low
                gm_ref[turn, j:j + 1, :] = taper * mean_gain
            end = 2 * width * members
            g_high, g_low = split(gm_ref[turn])
            lhs_ref[turn, end:end + 16, :] = jnp.concatenate([g_high, g_low], axis=0)
            product = lax.dot_general(
                lhs_ref[turn], anom_ref[...], (((1,), (1,)), ((), ())), preferred_element_type=F32
            )
            shift = product[end:end + 8, :PAD] + product[end:end + 8, PAD:] + product[end + 8:end + 16, :PAD]
            for j in range(width):
                first = product[2 * j * members:(2 * j + 1) * members]
                second = product[(2 * j + 1) * members:(2 * j + 2) * members, :PAD]
                spread = first[:, :PAD] + first[:, PAD:] + second
                x = g * width + j
                send_ref[slot, c, x, 0:mid, :] = jnp.where(
                    top_lane < members, spread[:mid], pltpu.roll(spread[mid:], mid, 1)
                )
                send_ref[slot, c, x, mid:mid + 8, :] = jnp.broadcast_to(shift[j:j + 1], (8, PAD))

        def contribute(c, turn):
            if nx == width:
                group(c, turn, 0)
            else:
                lax.fori_loop(0, nx // width, lambda g, carry: (group(c, turn, g), carry)[1], 0)

        contribute(other, 0)
        pair = remote(
            send_ref.at[slot, other], pair_ref.at[slot], pair_sem.at[slot, 0], pair_sem.at[slot, 1], (gx, other, ma)
        )
        pair.start()
        contribute(gy, 1)
        pair.wait()
        copies = []
        for d in list(range(1, nx)) + [0]:
            x = lax.rem(gx + d, nx)
            if d == 0:
                line_ref[slot, gx] = send_ref[slot, gy, gx] + pair_ref[slot, gx]
                continue
            send_ref[slot, gy, x] = send_ref[slot, gy, x] + pair_ref[slot, x]
            copy = remote(
                send_ref.at[slot, gy, x], line_ref.at[slot, gx],
                line_send.at[slot, d], line_recv.at[slot, gx], (x, gy, ma),
            )
            copy.start()
            copies.append((copy, remote(
                send_ref.at[slot, gy, x], line_ref.at[slot, x],
                line_send.at[slot, d], line_recv.at[slot, x], (x, gy, ma),
            )))

        if k + 1 < blocks:
            make_hot(k + 1)
            base, high, low = pick()
        else:
            base, high, low = flat_ref[...], split_ref[0:members, :], split_ref[members:2 * members, :]
        if k:
            if k == 1:
                change = mixing
            else:
                change = change + mixing + apply(mixing, *split(change))
            base = base + apply(change, high, low)
            high, low = split(base)
        if k + 1 == blocks:
            base = own_rows(base)

        for sent, received in copies:
            sent.wait_send()
            received.wait_recv()
        total = line_ref[slot, 0]
        for x in range(1, nx):
            total = total + line_ref[slot, x]
        top = total[:mid]
        turned = jnp.concatenate([top, jnp.zeros((PAD - mid, PAD), F32)], axis=0).T
        bottom = jnp.where(top_lane < mid, turned[mid:members], pltpu.roll(top, PAD - mid, 1))
        mixing = total[mid:mid + 1] - jnp.concatenate([top, bottom], axis=0)
        mixing = jnp.where(lane < members, mixing, 0.0)
        centre = jnp.sum(mixing, axis=1, keepdims=True) / members
        mixing = jnp.where(lane < members, mixing - centre, 0.0)
        if k + 1 < blocks:
            prior = base + apply(mixing, high, low)

    mine = base + apply(own_rows(mixing), high, low)
    for lev in range(levels):
        for x in range(cx):
            s = lev * cx + x
            out_ref[:, lev, x, :] = mine[0:members_dev, s * cy:(s + 1) * cy]


def local(
    ensemble, wind_field, obs_value, obs_var, obs_region, obs_cell, block_order, localization
):
    nx, ny, nm = lax.axis_size("gx"), lax.axis_size("gy"), lax.axis_size("ma")
    members_dev, levels, cx, cy = ensemble.shape
    half = members_dev // 2
    members = members_dev * nm
    blocks, obs = obs_value.shape
    rows = levels * cx
    cells = rows * cy
    regions = nx * ny
    width = 4 if nx % 4 == 0 else nx
    dma = pltpu.SemaphoreType.DMA
    vmem = pl.BlockSpec(memory_space=pltpu.VMEM)
    return pl.pallas_call(
        functools.partial(kernel, nx, ny, nm),
        out_shape=jax.ShapeDtypeStruct(ensemble.shape, F32),
        in_specs=[pl.BlockSpec(memory_space=pltpu.SMEM)] + [vmem] * 7,
        out_specs=vmem,
        scratch_shapes=[
            pltpu.VMEM((half, levels, cx, cy), F32),
            pltpu.VMEM(wind_field.shape, F32),
            pltpu.VMEM((ny, half + 2, 2 * levels, cy), F32),
            pltpu.VMEM((ny, half + 2, 2 * levels, cy), F32),
            pltpu.VMEM((ny, half + 2, 2 * levels, cy), F32),
            pltpu.VMEM((ny, half + 2, 2 * levels, cy), F32),
            pltpu.VMEM((half + 2, levels, cx + 4, 2 * cy), F32),
            pltpu.VMEM((ny, half, rows, cy), F32),
            pltpu.VMEM((members, rows, cy), F32),
            pltpu.VMEM((members, cells), F32),
            pltpu.VMEM((2 * members, cells), BF),
            pltpu.VMEM((regions, blocks, obs), F32),
            pltpu.VMEM((cells, obs), BF),
            pltpu.VMEM((2, 2 * width * members + 16, obs), BF),
            pltpu.VMEM((2, 8, obs), F32),
            pltpu.VMEM((2 * PAD, obs), BF),
            pltpu.VMEM((2, ny, nx, members // 2 + 8, PAD), F32),
            pltpu.VMEM((2, nx, members // 2 + 8, PAD), F32),
            pltpu.VMEM((2, nx, members // 2 + 8, PAD), F32),
            dma((4,)),
            dma((2, ny)),
            dma((2, ny)),
            dma((regions,)),
            dma((regions,)),
            dma((nm * ny,)),
            dma((nm * ny,)),
            dma((2, 2)),
            dma((2, nx)),
            dma((2, nx)),
        ],
        compiler_params=pltpu.CompilerParams(
            collective_id=0, has_side_effects=True, vmem_limit_bytes=56 * 1024 * 1024
        ),
    )(block_order, ensemble, wind_field, obs_value, obs_var, obs_region, obs_cell, localization)


def solution(mesh):
    in_specs = (
        P("ma", None, "gx", "gy"),
        P(None, None, "gx", "gy"),
        P(),
        P(),
        P(),
        P(),
        P(),
        P("gx", "gy", None, None),
    )
    out_specs = P("ma", None, "gx", "gy")
    return jax.shard_map(local, mesh=mesh, in_specs=in_specs, out_specs=out_specs, check_vma=False)
```

```python
import functools

import jax
import jax.numpy as jnp
from jax import lax
from jax.experimental import pallas as pl
from jax.experimental.pallas import tpu as pltpu
from jax.sharding import PartitionSpec as P

STEPS = 2
KAPPA = 0.025
PAD = 128
MESH = pl.DeviceIdType.MESH
BF = jnp.bfloat16
F32 = jnp.float32


def split(x):
    high = x.astype(BF)
    return high, (x - high.astype(F32)).astype(BF)


def kernel(
    nx, ny, nm,
    order_ref, ens_ref, wind_ref, value_ref, var_ref, region_ref, cell_ref, loc_ref,
    out_ref,
    o_ens, o_wind, up_ref, down_ref, low_ref, high_ref, ext_ref, piece_ref,
    all_ref, flat_ref, split_ref, loc_all, hot_ref, lhs_ref, next_ref, anom_ref,
    send_ref, pair_ref, line_ref,
    swap_sem, halo_send, halo_recv, loc_send, loc_recv, plane_send, plane_recv,
    pair_sem, line_send, line_recv,
):
    members_dev, levels, cx, cy = ens_ref.shape
    half = members_dev // 2
    members = members_dev * nm
    mid = members // 2
    blocks, obs = value_ref.shape
    cells = levels * cx * cy
    rows = levels * cx
    gx, gy, ma = lax.axis_index("gx"), lax.axis_index("gy"), lax.axis_index("ma")
    other = 1 - gy

    def remote(src, dst, send_sem, recv_sem, device):
        return pltpu.make_async_remote_copy(
            src_ref=src, dst_ref=dst, send_sem=send_sem, recv_sem=recv_sem,
            device_id=device, device_id_type=MESH,
        )

    line = [(lax.rem(gx + d, nx), c) for d in range(nx) for c in range(ny) if d or c]
    line = [(x, lax.rem(gy + c, ny)) for x, c in line]
    plane = [(lax.rem(ma + d, nm), lax.rem(gy + c, ny)) for d in range(nm) for c in range(ny) if d or c]

    barrier = pltpu.get_barrier_semaphore()
    for x, c in line:
        pl.semaphore_signal(barrier, inc=1, device_id=(x, c, ma), device_id_type=MESH)
    for m, c in plane[ny - 1:]:
        pl.semaphore_signal(barrier, inc=1, device_id=(gx, c, m), device_id_type=MESH)

    for c in range(ny):
        for lev in range(levels):
            pair_rows = slice(2 * lev, 2 * lev + 2)
            part = ens_ref[c * half:(c + 1) * half, lev]
            winds = wind_ref[:, lev]
            up_ref[c, 0:half, pair_rows, :] = part[:, cx - 2:cx]
            up_ref[c, half:half + 2, pair_rows, :] = winds[:, cx - 2:cx]
            down_ref[c, 0:half, pair_rows, :] = part[:, 0:2]
            down_ref[c, half:half + 2, pair_rows, :] = winds[:, 0:2]
    anom_ref[...] = jnp.zeros_like(anom_ref)

    pl.semaphore_wait(barrier, len(line) + len(plane) - (ny - 1))

    after, before = lax.rem(gx + 1, nx), lax.rem(gx + nx - 1, nx)
    halo = []
    for c in range(ny):
        for way, (src, dst, to, source) in enumerate(
            ((up_ref, low_ref, after, before), (down_ref, high_ref, before, after))
        ):
            copy = remote(src.at[c], dst.at[gy], halo_send.at[way, c], halo_recv.at[way, gy], (to, c, ma))
            copy.start()
            halo.append((copy, remote(
                src.at[c], dst.at[c], halo_send.at[way, c], halo_recv.at[way, c], (source, c, ma)
            )))
    swap = [
        remote(ens_ref.at[pl.ds(other * half, half)], o_ens, swap_sem.at[0], swap_sem.at[1], (gx, other, ma)),
        remote(wind_ref, o_wind, swap_sem.at[2], swap_sem.at[3], (gx, other, ma)),
    ]
    for copy in swap:
        copy.start()

    own_region = gx * ny + gy
    loc_copies = []
    for i, (x, c) in enumerate(line):
        source = x * ny + c
        copy = remote(loc_ref.at[0, 0], loc_all.at[own_region], loc_send.at[i], loc_recv.at[own_region], (x, c, ma))
        copy.start()
        loc_copies.append((copy, remote(loc_ref.at[0, 0], loc_all.at[source], loc_send.at[i], loc_recv.at[source], (x, c, ma))))
    loc_all[own_region] = loc_ref[0, 0]

    def make_hot(k):
        b = order_ref[k]
        cell = jnp.where(region_ref[pl.ds(b, 1), :] == own_region, cell_ref[pl.ds(b, 1), :], -1)
        for s in range(cells // PAD):
            index = lax.broadcasted_iota(jnp.int32, (PAD, obs), 0) + s * PAD
            hot_ref[k, s * PAD:(s + 1) * PAD, :] = jnp.where(index == cell, 1.0, 0.0).astype(BF)

    make_hot(0)
    make_hot(1)
    for copy in swap:
        copy.wait()

    left = gy == 0
    own_t = ens_ref[pl.ds(gy * half, half)]
    for lev in range(levels):
        pairs = (
            (own_t[:, lev], o_ens[:, lev], slice(0, half)),
            (wind_ref[:, lev], o_wind[:, lev], slice(half, half + 2)),
        )
        for mine, theirs, where in pairs:
            ext_ref[where, lev, 2:2 + cx, 0:cy] = jnp.where(left, mine, theirs)
            ext_ref[where, lev, 2:2 + cx, cy:2 * cy] = jnp.where(left, theirs, mine)
    for sent, received in halo:
        sent.wait_send()
        received.wait_recv()

    for lev in range(levels):
        for c in range(ny):
            lanes = slice(c * cy, (c + 1) * cy)
            ext_ref[:, lev, 0:2, lanes] = low_ref[c, :, 2 * lev:2 * lev + 2, :]
            ext_ref[:, lev, 2 + cx:4 + cx, lanes] = high_ref[c, :, 2 * lev:2 * lev + 2, :]
    for lev in range(levels):
        east_wind = ext_ref[half, lev][None]
        north_wind = ext_ref[half + 1, lev][None]
        q = ext_ref[0:half, lev]
        for _ in range(STEPS):
            west = pltpu.roll(q, 1, 1)
            east = pltpu.roll(q, cx + 3, 1)
            south = pltpu.roll(q, 1, 2)
            north = pltpu.roll(q, 2 * cy - 1, 2)
            q = (
                q
                - jnp.maximum(east_wind, 0.0) * (q - west)
                - jnp.minimum(east_wind, 0.0) * (east - q)
                - jnp.maximum(north_wind, 0.0) * (q - south)
                - jnp.minimum(north_wind, 0.0) * (north - q)
                + KAPPA * (east + west + north + south - 4.0 * q)
            )
        for c in range(ny):
            piece_ref[c, :, lev * cx:(lev + 1) * cx, :] = q[:, 2:2 + cx, c * cy:(c + 1) * cy]

    own_part = ma * ny + gy
    plane_copies = []
    for i, (m, c) in enumerate(plane):
        source = m * ny + c
        copy = remote(
            piece_ref.at[c], all_ref.at[pl.ds(own_part * half, half)],
            plane_send.at[i], plane_recv.at[own_part], (gx, c, m),
        )
        copy.start()
        plane_copies.append((copy, remote(
            piece_ref.at[gy], all_ref.at[pl.ds(source * half, half)],
            plane_send.at[i], plane_recv.at[source], (gx, c, m),
        )))
    all_ref[pl.ds(own_part * half, half)] = piece_ref[gy]
    for k in range(2, blocks):
        make_hot(k)
    for sent, received in plane_copies:
        sent.wait_send()
        received.wait_recv()

    for s in range(rows):
        lanes = slice(s * cy, (s + 1) * cy)
        values = all_ref[:, s, :]
        flat_ref[:, lanes] = values
        high, low = split(values)
        split_ref[0:members, lanes] = high
        split_ref[members:2 * members, lanes] = low

    def pick(k):
        both = jnp.dot(split_ref[...], hot_ref[k], preferred_element_type=F32)
        return both[:members] + both[members:], both[:members].astype(BF), both[members:].astype(BF)

    def stack(high, low):
        return jnp.concatenate([high, low, high], axis=0)

    def apply(change, stacked):
        high = change.astype(BF).astype(F32)
        blank = jnp.zeros_like(change)
        high, low = (jnp.concatenate([part, blank], axis=1) for part in (high, change - high))
        wide = high + pltpu.roll(high, members, 1) + pltpu.roll(low, 2 * members, 1)
        return jnp.dot(wide.astype(BF)[:, :3 * members], stacked, preferred_element_type=F32)

    def own_rows(x):
        own = x[0:members_dev]
        for m in range(1, nm):
            own = jnp.where(ma == m, x[m * members_dev:(m + 1) * members_dev], own)
        filler = jnp.zeros((-members_dev % 16, x.shape[1]), F32)
        return jnp.concatenate([own, filler], axis=0)

    width = 4 if nx % 4 == 0 else nx
    lane = lax.broadcasted_iota(jnp.int32, (members, PAD), 1)
    top_lane = lane[:mid]
    denom = members - 1.0
    prior = pick(0)[0]
    for sent, received in loc_copies:
        sent.wait_send()
        received.wait_recv()

    change = mixing = None
    for k in range(blocks):
        slot = k % 2
        b = order_ref[k]
        error_var = var_ref[pl.ds(b, 1), :]
        obs_mean = jnp.sum(prior, axis=0, keepdims=True) / members
        anomaly = prior - obs_mean
        variance = jnp.sum(anomaly * anomaly, axis=0, keepdims=True) / denom
        total_var = variance + error_var
        innovation = value_ref[pl.ds(b, 1), :] - obs_mean
        shrink = 1.0 / (1.0 + jnp.sqrt(error_var / total_var))
        scaled = 1.0 / (denom * total_var)
        lift = innovation * (1.0 + jnp.sqrt(error_var / total_var))
        spread_gain = shrink * scaled
        a_high, a_low = split(anomaly)
        anom_ref[0:members, :] = a_high
        anom_ref[PAD:PAD + members, :] = a_low
        lift_high, lift_low = split(jnp.concatenate([lift, jnp.zeros((15, obs), F32)], axis=0))
        anom_ref[members:members + 16, :] = lift_high
        anom_ref[PAD + members:PAD + members + 16, :] = lift_low

        def group(c, turn, g):
            for j in range(width):
                taper = loc_all[(g * width + j) * ny + c, pl.ds(b, 1), :]
                w_high, w_low = split(anomaly * (taper * spread_gain))
                lhs_ref[turn, 2 * j * members:(2 * j + 1) * members, :] = w_high
                lhs_ref[turn, (2 * j + 1) * members:(2 * j + 2) * members, :] = w_low
            product = lax.dot_general(
                lhs_ref[turn], anom_ref[...], (((1,), (1,)), ((), ())), preferred_element_type=F32
            )
            for j in range(width):
                first = product[2 * j * members:(2 * j + 1) * members]
                second = product[(2 * j + 1) * members:(2 * j + 2) * members, :PAD]
                spread = first[:, :PAD] + first[:, PAD:] + second
                x = g * width + j
                packed = jnp.where(top_lane < members, spread[:mid], pltpu.roll(spread[mid:], mid, 1))
                last = members + mid + 1
                send_ref[slot, c, x] = jnp.where(top_lane == last, pltpu.roll(spread[:mid], mid + 1, 1), packed)

        def contribute(c, turn):
            if nx == width:
                group(c, turn, 0)
            else:
                lax.fori_loop(0, nx // width, lambda g, carry: (group(c, turn, g), carry)[1], 0)

        contribute(other, 0)
        pair = remote(
            send_ref.at[slot, other], pair_ref.at[slot], pair_sem.at[slot, 0], pair_sem.at[slot, 1], (gx, other, ma)
        )
        pair.start()
        contribute(gy, 1)
        pair.wait()
        copies = []
        for d in list(range(1, nx)) + [0]:
            x = lax.rem(gx + d, nx)
            if d == 0:
                line_ref[slot, gx] = send_ref[slot, gy, gx] + pair_ref[slot, gx]
                continue
            send_ref[slot, gy, x] = send_ref[slot, gy, x] + pair_ref[slot, x]
            copy = remote(
                send_ref.at[slot, gy, x], line_ref.at[slot, gx],
                line_send.at[slot, d], line_recv.at[slot, gx], (x, gy, ma),
            )
            copy.start()
            copies.append((copy, remote(
                send_ref.at[slot, gy, x], line_ref.at[slot, x],
                line_send.at[slot, d], line_recv.at[slot, x], (x, gy, ma),
            )))

        if k + 1 < blocks:
            base, high, low = pick(k + 1)
        else:
            base, high, low = flat_ref[...], split_ref[0:members, :], split_ref[members:2 * members, :]
        if k:
            if k == 1:
                change = mixing
            else:
                change = change + mixing + apply(mixing, stack(*split(change)))
            base = base + apply(change, stack(high, low))
            high, low = split(base)
        next_ref[...] = stack(high, low)
        if k + 1 == blocks:
            base = own_rows(base)

        for sent, received in copies:
            sent.wait_send()
            received.wait_recv()
        total = line_ref[slot, 0]
        for x in range(1, nx):
            total = total + line_ref[slot, x]
        top = total
        turned = jnp.concatenate([top, jnp.zeros((PAD - mid, PAD), F32)], axis=0).T
        bottom = jnp.where(top_lane < mid, turned[mid:members], pltpu.roll(top, PAD - mid, 1))
        last = members + mid
        shift = turned[last + 1:last + 2] + pltpu.roll(turned[last:last + 8], mid, 1)[0:1]
        mixing = shift - jnp.concatenate([top, bottom], axis=0)
        mixing = jnp.where(lane < members, mixing, 0.0)
        centre = jnp.sum(mixing, axis=1, keepdims=True) / members
        mixing = jnp.where(lane < members, mixing - centre, 0.0)
        if k + 1 < blocks:
            prior = base + apply(mixing, next_ref[...])

    mine = base + apply(own_rows(mixing), next_ref[...])
    for lev in range(levels):
        for x in range(cx):
            s = lev * cx + x
            out_ref[:, lev, x, :] = mine[0:members_dev, s * cy:(s + 1) * cy]


def local(
    ensemble, wind_field, obs_value, obs_var, obs_region, obs_cell, block_order, localization
):
    nx, ny, nm = lax.axis_size("gx"), lax.axis_size("gy"), lax.axis_size("ma")
    members_dev, levels, cx, cy = ensemble.shape
    half = members_dev // 2
    members = members_dev * nm
    blocks, obs = obs_value.shape
    rows = levels * cx
    cells = rows * cy
    regions = nx * ny
    width = 4 if nx % 4 == 0 else nx
    dma = pltpu.SemaphoreType.DMA
    vmem = pl.BlockSpec(memory_space=pltpu.VMEM)
    return pl.pallas_call(
        functools.partial(kernel, nx, ny, nm),
        out_shape=jax.ShapeDtypeStruct(ensemble.shape, F32),
        in_specs=[pl.BlockSpec(memory_space=pltpu.SMEM)] + [vmem] * 7,
        out_specs=vmem,
        scratch_shapes=[
            pltpu.VMEM((half, levels, cx, cy), F32),
            pltpu.VMEM(wind_field.shape, F32),
            pltpu.VMEM((ny, half + 2, 2 * levels, cy), F32),
            pltpu.VMEM((ny, half + 2, 2 * levels, cy), F32),
            pltpu.VMEM((ny, half + 2, 2 * levels, cy), F32),
            pltpu.VMEM((ny, half + 2, 2 * levels, cy), F32),
            pltpu.VMEM((half + 2, levels, cx + 4, 2 * cy), F32),
            pltpu.VMEM((ny, half, rows, cy), F32),
            pltpu.VMEM((members, rows, cy), F32),
            pltpu.VMEM((members, cells), F32),
            pltpu.VMEM((2 * members, cells), BF),
            pltpu.VMEM((regions, blocks, obs), F32),
            pltpu.VMEM((blocks, cells, obs), BF),
            pltpu.VMEM((2, 2 * width * members, obs), BF),
            pltpu.VMEM((3 * members, cells), BF),
            pltpu.VMEM((2 * PAD, obs), BF),
            pltpu.VMEM((2, ny, nx, members // 2, PAD), F32),
            pltpu.VMEM((2, nx, members // 2, PAD), F32),
            pltpu.VMEM((2, nx, members // 2, PAD), F32),
            dma((4,)),
            dma((2, ny)),
            dma((2, ny)),
            dma((regions,)),
            dma((regions,)),
            dma((nm * ny,)),
            dma((nm * ny,)),
            dma((2, 2)),
            dma((2, nx)),
            dma((2, nx)),
        ],
        compiler_params=pltpu.CompilerParams(
            collective_id=0, has_side_effects=True, vmem_limit_bytes=56 * 1024 * 1024
        ),
    )(block_order, ensemble, wind_field, obs_value, obs_var, obs_region, obs_cell, localization)


def solution(mesh):
    in_specs = (
        P("ma", None, "gx", "gy"),
        P(None, None, "gx", "gy"),
        P(),
        P(),
        P(),
        P(),
        P(),
        P("gx", "gy", None, None),
    )
    out_specs = P("ma", None, "gx", "gy")
    return jax.shard_map(local, mesh=mesh, in_specs=in_specs, out_specs=out_specs, check_vma=False)
```

```python
import functools

import jax
import jax.numpy as jnp
from jax import lax
from jax.experimental import pallas as pl
from jax.experimental.pallas import tpu as pltpu
from jax.sharding import PartitionSpec as P

STEPS = 2
KAPPA = 0.025
PAD = 128
MESH = pl.DeviceIdType.MESH
BF = jnp.bfloat16
F32 = jnp.float32


def split(x):
    high = x.astype(BF)
    return high, (x - high.astype(F32)).astype(BF)


def kernel(
    nx, ny, nm,
    order_ref, ens_in, wind_in, value_in, var_in, region_in, cell_in, loc_in,
    out_ref,
    ens_ref, wind_ref, value_ref, var_ref, region_ref, cell_ref, loc_ref, in_sem,
    o_ens, o_wind, up_ref, down_ref, low_ref, high_ref, ext_ref, piece_ref,
    all_ref, flat_ref, split_ref, loc_all, hot_ref, lhs_ref, next_ref, anom_ref,
    send_ref, pair_ref, line_ref,
    swap_sem, halo_send, halo_recv, loc_send, loc_recv, plane_send, plane_recv,
    pair_sem, line_send, line_recv,
):
    members_dev, levels, cx, cy = ens_ref.shape
    half = members_dev // 2
    members = members_dev * nm
    mid = members // 2
    blocks, obs = value_ref.shape
    cells = levels * cx * cy
    rows = levels * cx
    gx, gy, ma = lax.axis_index("gx"), lax.axis_index("gy"), lax.axis_index("ma")
    other = 1 - gy

    def remote(src, dst, send_sem, recv_sem, device):
        return pltpu.make_async_remote_copy(
            src_ref=src, dst_ref=dst, send_sem=send_sem, recv_sem=recv_sem,
            device_id=device, device_id_type=MESH,
        )

    line = [(lax.rem(gx + d, nx), c) for d in range(nx) for c in range(ny) if d or c]
    line = [(x, lax.rem(gy + c, ny)) for x, c in line]
    plane = [(lax.rem(ma + d, nm), lax.rem(gy + c, ny)) for d in range(nm) for c in range(ny) if d or c]

    barrier = pltpu.get_barrier_semaphore()
    for x, c in line:
        pl.semaphore_signal(barrier, inc=1, device_id=(x, c, ma), device_id_type=MESH)
    for m, c in plane[ny - 1:]:
        pl.semaphore_signal(barrier, inc=1, device_id=(gx, c, m), device_id_type=MESH)

    inputs = [
        pltpu.make_async_copy(src, dst, in_sem.at[i])
        for i, (src, dst) in enumerate((
            (ens_in, ens_ref), (wind_in, wind_ref), (region_in, region_ref), (cell_in, cell_ref),
            (loc_in, loc_ref), (value_in, value_ref), (var_in, var_ref),
        ))
    ]
    for copy in inputs:
        copy.start()
    for copy in inputs[:2]:
        copy.wait()

    for c in range(ny):
        for lev in range(levels):
            pair_rows = slice(2 * lev, 2 * lev + 2)
            part = ens_ref[c * half:(c + 1) * half, lev]
            winds = wind_ref[:, lev]
            up_ref[c, 0:half, pair_rows, :] = part[:, cx - 2:cx]
            up_ref[c, half:half + 2, pair_rows, :] = winds[:, cx - 2:cx]
            down_ref[c, 0:half, pair_rows, :] = part[:, 0:2]
            down_ref[c, half:half + 2, pair_rows, :] = winds[:, 0:2]
    anom_ref[...] = jnp.zeros_like(anom_ref)

    for copy in inputs[2:]:
        copy.wait()
    pl.semaphore_wait(barrier, len(line) + len(plane) - (ny - 1))

    after, before = lax.rem(gx + 1, nx), lax.rem(gx + nx - 1, nx)
    halo = []
    for c in range(ny):
        for way, (src, dst, to, source) in enumerate(
            ((up_ref, low_ref, after, before), (down_ref, high_ref, before, after))
        ):
            copy = remote(src.at[c], dst.at[gy], halo_send.at[way, c], halo_recv.at[way, gy], (to, c, ma))
            copy.start()
            halo.append((copy, remote(
                src.at[c], dst.at[c], halo_send.at[way, c], halo_recv.at[way, c], (source, c, ma)
            )))
    swap = [
        remote(ens_ref.at[pl.ds(other * half, half)], o_ens, swap_sem.at[0], swap_sem.at[1], (gx, other, ma)),
        remote(wind_ref, o_wind, swap_sem.at[2], swap_sem.at[3], (gx, other, ma)),
    ]
    for copy in swap:
        copy.start()

    own_region = gx * ny + gy
    loc_copies = []
    for i, (x, c) in enumerate(line):
        source = x * ny + c
        copy = remote(loc_ref.at[0, 0], loc_all.at[own_region], loc_send.at[i], loc_recv.at[own_region], (x, c, ma))
        copy.start()
        loc_copies.append((copy, remote(loc_ref.at[0, 0], loc_all.at[source], loc_send.at[i], loc_recv.at[source], (x, c, ma))))
    loc_all[own_region] = loc_ref[0, 0]

    def make_hot(k):
        b = order_ref[k]
        cell = jnp.where(region_ref[pl.ds(b, 1), :] == own_region, cell_ref[pl.ds(b, 1), :], -1)
        for s in range(cells // PAD):
            index = lax.broadcasted_iota(jnp.int32, (PAD, obs), 0) + s * PAD
            hot_ref[k, s * PAD:(s + 1) * PAD, :] = jnp.where(index == cell, 1.0, 0.0).astype(BF)

    make_hot(0)
    make_hot(1)
    for copy in swap:
        copy.wait()

    left = gy == 0
    own_t = ens_ref[pl.ds(gy * half, half)]
    for lev in range(levels):
        pairs = (
            (own_t[:, lev], o_ens[:, lev], slice(0, half)),
            (wind_ref[:, lev], o_wind[:, lev], slice(half, half + 2)),
        )
        for mine, theirs, where in pairs:
            ext_ref[where, lev, 2:2 + cx, 0:cy] = jnp.where(left, mine, theirs)
            ext_ref[where, lev, 2:2 + cx, cy:2 * cy] = jnp.where(left, theirs, mine)
    for sent, received in halo:
        sent.wait_send()
        received.wait_recv()

    for lev in range(levels):
        for c in range(ny):
            lanes = slice(c * cy, (c + 1) * cy)
            ext_ref[:, lev, 0:2, lanes] = low_ref[c, :, 2 * lev:2 * lev + 2, :]
            ext_ref[:, lev, 2 + cx:4 + cx, lanes] = high_ref[c, :, 2 * lev:2 * lev + 2, :]
    for lev in range(levels):
        east_wind = ext_ref[half, lev][None]
        north_wind = ext_ref[half + 1, lev][None]
        q = ext_ref[0:half, lev]
        for _ in range(STEPS):
            west = pltpu.roll(q, 1, 1)
            east = pltpu.roll(q, cx + 3, 1)
            south = pltpu.roll(q, 1, 2)
            north = pltpu.roll(q, 2 * cy - 1, 2)
            q = (
                q
                - jnp.maximum(east_wind, 0.0) * (q - west)
                - jnp.minimum(east_wind, 0.0) * (east - q)
                - jnp.maximum(north_wind, 0.0) * (q - south)
                - jnp.minimum(north_wind, 0.0) * (north - q)
                + KAPPA * (east + west + north + south - 4.0 * q)
            )
        for c in range(ny):
            piece_ref[c, :, lev * cx:(lev + 1) * cx, :] = q[:, 2:2 + cx, c * cy:(c + 1) * cy]

    own_part = ma * ny + gy
    plane_copies = []
    for i, (m, c) in enumerate(plane):
        source = m * ny + c
        copy = remote(
            piece_ref.at[c], all_ref.at[pl.ds(own_part * half, half)],
            plane_send.at[i], plane_recv.at[own_part], (gx, c, m),
        )
        copy.start()
        plane_copies.append((copy, remote(
            piece_ref.at[gy], all_ref.at[pl.ds(source * half, half)],
            plane_send.at[i], plane_recv.at[source], (gx, c, m),
        )))
    all_ref[pl.ds(own_part * half, half)] = piece_ref[gy]
    for k in range(2, blocks):
        make_hot(k)
    for sent, received in plane_copies:
        sent.wait_send()
        received.wait_recv()

    for s in range(rows):
        lanes = slice(s * cy, (s + 1) * cy)
        values = all_ref[:, s, :]
        flat_ref[:, lanes] = values
        high, low = split(values)
        split_ref[0:members, lanes] = high
        split_ref[members:2 * members, lanes] = low

    def pick(k):
        both = jnp.dot(split_ref[...], hot_ref[k], preferred_element_type=F32)
        return both[:members] + both[members:], both[:members].astype(BF), both[members:].astype(BF)

    def stack(high, low):
        return jnp.concatenate([high, low, high], axis=0)

    def apply(change, stacked):
        high = change.astype(BF).astype(F32)
        blank = jnp.zeros_like(change)
        high, low = (jnp.concatenate([part, blank], axis=1) for part in (high, change - high))
        wide = high + pltpu.roll(high, members, 1) + pltpu.roll(low, 2 * members, 1)
        return jnp.dot(wide.astype(BF)[:, :3 * members], stacked, preferred_element_type=F32)

    def own_rows(x):
        own = x[0:members_dev]
        for m in range(1, nm):
            own = jnp.where(ma == m, x[m * members_dev:(m + 1) * members_dev], own)
        filler = jnp.zeros((-members_dev % 16, x.shape[1]), F32)
        return jnp.concatenate([own, filler], axis=0)

    lane = lax.broadcasted_iota(jnp.int32, (members, PAD), 1)
    top_lane = lane[:mid]
    denom = members - 1.0
    prior = pick(0)[0]
    for sent, received in loc_copies:
        sent.wait_send()
        received.wait_recv()

    change = mixing = None
    for k in range(blocks):
        slot = k % 2
        b = order_ref[k]
        error_var = var_ref[pl.ds(b, 1), :]
        obs_mean = jnp.sum(prior, axis=0, keepdims=True) / members
        anomaly = prior - obs_mean
        variance = jnp.sum(anomaly * anomaly, axis=0, keepdims=True) / denom
        total_var = variance + error_var
        innovation = value_ref[pl.ds(b, 1), :] - obs_mean
        shrink = 1.0 / (1.0 + jnp.sqrt(error_var / total_var))
        scaled = 1.0 / (denom * total_var)
        lift = innovation * (1.0 + jnp.sqrt(error_var / total_var))
        spread_gain = shrink * scaled
        a_high, a_low = split(anomaly)
        anom_ref[0:members, :] = a_high
        anom_ref[PAD:PAD + members, :] = a_low
        lift_high, lift_low = split(jnp.concatenate([lift, jnp.zeros((15, obs), F32)], axis=0))
        anom_ref[members:members + 16, :] = lift_high
        anom_ref[PAD + members:PAD + members + 16, :] = lift_low

        def pair_copy(x):
            return remote(
                send_ref.at[slot, other, x], pair_ref.at[slot, x],
                pair_sem.at[slot, 0, x], pair_sem.at[slot, 1, x], (gx, other, ma),
            )

        def line_copy(x, place):
            return remote(
                send_ref.at[slot, gy, x], line_ref.at[slot, place],
                line_send.at[slot, x], line_recv.at[slot, place], (x, gy, ma),
            )

        def terms(x, turn):
            for c in range(ny):
                taper = loc_all[x * ny + c, pl.ds(b, 1), :]
                w_high, w_low = split(anomaly * (taper * spread_gain))
                lhs_ref[turn, 2 * c * members:(2 * c + 1) * members, :] = w_high
                lhs_ref[turn, (2 * c + 1) * members:(2 * c + 2) * members, :] = w_low
            product = lax.dot_general(
                lhs_ref[turn], anom_ref[...], (((1,), (1,)), ((), ())), preferred_element_type=F32
            )
            for c in range(ny):
                first = product[2 * c * members:(2 * c + 1) * members]
                second = product[(2 * c + 1) * members:(2 * c + 2) * members, :PAD]
                spread = first[:, :PAD] + first[:, PAD:] + second
                packed = jnp.where(top_lane < members, spread[:mid], pltpu.roll(spread[mid:], mid, 1))
                last = members + mid + 1
                send_ref[slot, c, x] = jnp.where(top_lane == last, pltpu.roll(spread[:mid], mid + 1, 1), packed)
            pair_copy(x).start()

        def forward(x, away):
            pair_copy(x).wait()
            both = send_ref[slot, gy, x] + pair_ref[slot, x]
            if away:
                send_ref[slot, gy, x] = both
                line_copy(x, gx).start()
            else:
                line_ref[slot, x] = both

        ahead = [lax.rem(gx + d, nx) for d in range(nx)]
        if nx <= 8:
            order = ahead[2:3] + ahead[1:2] + ahead[3:] + ahead[:1]
            for i, x in enumerate(order):
                terms(x, i % 2)
                if i:
                    forward(order[i - 1], True)
        else:
            def step(d, carry):
                terms(lax.rem(gx + d, nx), 0)
                forward(lax.rem(gx + d, nx), True)
                return carry

            lax.fori_loop(1, nx, step, 0)
            terms(gx, 1)
        forward(gx, False)

        if k + 1 < blocks:
            base, high, low = pick(k + 1)
        else:
            base, high, low = flat_ref[...], split_ref[0:members, :], split_ref[members:2 * members, :]
        if k:
            if k == 1:
                change = mixing
            else:
                change = change + mixing + apply(mixing, stack(*split(change)))
            base = base + apply(change, stack(high, low))
            high, low = split(base)
        next_ref[...] = stack(high, low)
        if k + 1 == blocks:
            base = own_rows(base)

        for x in ahead[1:]:
            line_copy(x, gx).wait_send()
            line_copy(x, x).wait_recv()
        total = line_ref[slot, 0]
        for x in range(1, nx):
            total = total + line_ref[slot, x]
        top = total
        turned = jnp.concatenate([top, jnp.zeros((PAD - mid, PAD), F32)], axis=0).T
        bottom = jnp.where(top_lane < mid, turned[mid:members], pltpu.roll(top, PAD - mid, 1))
        last = members + mid
        shift = turned[last + 1:last + 2] + pltpu.roll(turned[last:last + 8], mid, 1)[0:1]
        mixing = shift - jnp.concatenate([top, bottom], axis=0)
        mixing = jnp.where(lane < members, mixing, 0.0)
        centre = jnp.sum(mixing, axis=1, keepdims=True) / members
        mixing = jnp.where(lane < members, mixing - centre, 0.0)
        if k + 1 < blocks:
            prior = base + apply(mixing, next_ref[...])

    mine = base + apply(own_rows(mixing), next_ref[...])
    for lev in range(levels):
        for x in range(cx):
            s = lev * cx + x
            out_ref[:, lev, x, :] = mine[0:members_dev, s * cy:(s + 1) * cy]


def local(
    ensemble, wind_field, obs_value, obs_var, obs_region, obs_cell, block_order, localization
):
    nx, ny, nm = lax.axis_size("gx"), lax.axis_size("gy"), lax.axis_size("ma")
    members_dev, levels, cx, cy = ensemble.shape
    half = members_dev // 2
    members = members_dev * nm
    blocks, obs = obs_value.shape
    rows = levels * cx
    cells = rows * cy
    regions = nx * ny
    dma = pltpu.SemaphoreType.DMA
    vmem = pl.BlockSpec(memory_space=pltpu.VMEM)
    return pl.pallas_call(
        functools.partial(kernel, nx, ny, nm),
        out_shape=jax.ShapeDtypeStruct(ensemble.shape, F32),
        in_specs=[pl.BlockSpec(memory_space=pltpu.SMEM)] + [pl.BlockSpec(memory_space=pl.ANY)] * 7,
        out_specs=vmem,
        scratch_shapes=[
            pltpu.VMEM(ensemble.shape, F32),
            pltpu.VMEM(wind_field.shape, F32),
            pltpu.VMEM(obs_value.shape, F32),
            pltpu.VMEM(obs_var.shape, F32),
            pltpu.VMEM(obs_region.shape, jnp.int32),
            pltpu.VMEM(obs_cell.shape, jnp.int32),
            pltpu.VMEM(localization.shape, F32),
            dma((7,)),
            pltpu.VMEM((half, levels, cx, cy), F32),
            pltpu.VMEM(wind_field.shape, F32),
            pltpu.VMEM((ny, half + 2, 2 * levels, cy), F32),
            pltpu.VMEM((ny, half + 2, 2 * levels, cy), F32),
            pltpu.VMEM((ny, half + 2, 2 * levels, cy), F32),
            pltpu.VMEM((ny, half + 2, 2 * levels, cy), F32),
            pltpu.VMEM((half + 2, levels, cx + 4, 2 * cy), F32),
            pltpu.VMEM((ny, half, rows, cy), F32),
            pltpu.VMEM((members, rows, cy), F32),
            pltpu.VMEM((members, cells), F32),
            pltpu.VMEM((2 * members, cells), BF),
            pltpu.VMEM((regions, blocks, obs), F32),
            pltpu.VMEM((blocks, cells, obs), BF),
            pltpu.VMEM((2, 2 * ny * members, obs), BF),
            pltpu.VMEM((3 * members, cells), BF),
            pltpu.VMEM((2 * PAD, obs), BF),
            pltpu.VMEM((2, ny, nx, members // 2, PAD), F32),
            pltpu.VMEM((2, nx, members // 2, PAD), F32),
            pltpu.VMEM((2, nx, members // 2, PAD), F32),
            dma((4,)),
            dma((2, ny)),
            dma((2, ny)),
            dma((regions,)),
            dma((regions,)),
            dma((nm * ny,)),
            dma((nm * ny,)),
            dma((2, 2, nx)),
            dma((2, nx)),
            dma((2, nx)),
        ],
        compiler_params=pltpu.CompilerParams(
            collective_id=0, has_side_effects=True, vmem_limit_bytes=56 * 1024 * 1024
        ),
    )(block_order, ensemble, wind_field, obs_value, obs_var, obs_region, obs_cell, localization)


def solution(mesh):
    in_specs = (
        P("ma", None, "gx", "gy"),
        P(None, None, "gx", "gy"),
        P(),
        P(),
        P(),
        P(),
        P(),
        P("gx", "gy", None, None),
    )
    out_specs = P("ma", None, "gx", "gy")
    return jax.shard_map(local, mesh=mesh, in_specs=in_specs, out_specs=out_specs, check_vma=False)
```

```python
import functools

import jax
import jax.numpy as jnp
from jax import lax
from jax.experimental import pallas as pl
from jax.experimental.pallas import tpu as pltpu
from jax.sharding import PartitionSpec as P

STEPS = 2
KAPPA = 0.025
PAD = 128
MESH = pl.DeviceIdType.MESH
BF = jnp.bfloat16
F32 = jnp.float32


def split(x):
    high = x.astype(BF)
    return high, (x - high.astype(F32)).astype(BF)


def kernel(
    nx, ny, nm,
    order_ref, ens_in, wind_in, value_in, var_in, region_in, cell_in, loc_in,
    out_ref,
    ens_ref, wind_ref, value_ref, var_ref, region_ref, cell_ref, loc_ref, in_sem,
    o_ens, o_wind, up_ref, down_ref, low_ref, high_ref, ext_ref, piece_ref,
    all_ref, flat_ref, split_ref, loc_all, hot_ref, lhs_ref, next_ref, anom_ref,
    send_ref, pair_ref, line_ref, base_ref, part_ref, prior_ref, mixing_ref, change_ref,
    swap_sem, halo_send, halo_recv, loc_send, loc_recv, plane_send, plane_recv,
    pair_sem, line_send, line_recv,
):
    members_dev, levels, cx, cy = ens_ref.shape
    half = members_dev // 2
    members = members_dev * nm
    mid = members // 2
    blocks, obs = value_ref.shape
    cells = levels * cx * cy
    rows = levels * cx
    gx, gy, ma = lax.axis_index("gx"), lax.axis_index("gy"), lax.axis_index("ma")
    other = 1 - gy

    def remote(src, dst, send_sem, recv_sem, device):
        return pltpu.make_async_remote_copy(
            src_ref=src, dst_ref=dst, send_sem=send_sem, recv_sem=recv_sem,
            device_id=device, device_id_type=MESH,
        )

    line = [(lax.rem(gx + d, nx), c) for d in range(nx) for c in range(ny) if d or c]
    line = [(x, lax.rem(gy + c, ny)) for x, c in line]
    plane = [(lax.rem(ma + d, nm), lax.rem(gy + c, ny)) for d in range(nm) for c in range(ny) if d or c]

    barrier = pltpu.get_barrier_semaphore()
    for x, c in line:
        pl.semaphore_signal(barrier, inc=1, device_id=(x, c, ma), device_id_type=MESH)
    for m, c in plane[ny - 1:]:
        pl.semaphore_signal(barrier, inc=1, device_id=(gx, c, m), device_id_type=MESH)

    inputs = [
        pltpu.make_async_copy(src, dst, in_sem.at[i])
        for i, (src, dst) in enumerate((
            (ens_in, ens_ref), (wind_in, wind_ref), (region_in, region_ref), (cell_in, cell_ref),
            (loc_in, loc_ref), (value_in, value_ref), (var_in, var_ref),
        ))
    ]
    for copy in inputs:
        copy.start()
    for copy in inputs[:2]:
        copy.wait()

    for c in range(ny):
        for lev in range(levels):
            pair_rows = slice(2 * lev, 2 * lev + 2)
            part = ens_ref[c * half:(c + 1) * half, lev]
            winds = wind_ref[:, lev]
            up_ref[c, 0:half, pair_rows, :] = part[:, cx - 2:cx]
            up_ref[c, half:half + 2, pair_rows, :] = winds[:, cx - 2:cx]
            down_ref[c, 0:half, pair_rows, :] = part[:, 0:2]
            down_ref[c, half:half + 2, pair_rows, :] = winds[:, 0:2]
    anom_ref[...] = jnp.zeros_like(anom_ref)

    for copy in inputs[2:]:
        copy.wait()
    pl.semaphore_wait(barrier, len(line) + len(plane) - (ny - 1))

    after, before = lax.rem(gx + 1, nx), lax.rem(gx + nx - 1, nx)
    halo = []
    for c in range(ny):
        for way, (src, dst, to, source) in enumerate(
            ((up_ref, low_ref, after, before), (down_ref, high_ref, before, after))
        ):
            copy = remote(src.at[c], dst.at[gy], halo_send.at[way, c], halo_recv.at[way, gy], (to, c, ma))
            copy.start()
            halo.append((copy, remote(
                src.at[c], dst.at[c], halo_send.at[way, c], halo_recv.at[way, c], (source, c, ma)
            )))
    swap = [
        remote(ens_ref.at[pl.ds(other * half, half)], o_ens, swap_sem.at[0], swap_sem.at[1], (gx, other, ma)),
        remote(wind_ref, o_wind, swap_sem.at[2], swap_sem.at[3], (gx, other, ma)),
    ]
    for copy in swap:
        copy.start()

    own_region = gx * ny + gy
    loc_copies = []
    for i, (x, c) in enumerate(line):
        source = x * ny + c
        copy = remote(loc_ref.at[0, 0], loc_all.at[own_region], loc_send.at[i], loc_recv.at[own_region], (x, c, ma))
        copy.start()
        loc_copies.append((copy, remote(loc_ref.at[0, 0], loc_all.at[source], loc_send.at[i], loc_recv.at[source], (x, c, ma))))
    loc_all[own_region] = loc_ref[0, 0]

    def make_hot(k, carry):
        b = order_ref[k]
        cell = jnp.where(region_ref[pl.ds(b, 1), :] == own_region, cell_ref[pl.ds(b, 1), :], -1)
        for s in range(cells // PAD):
            index = lax.broadcasted_iota(jnp.int32, (PAD, obs), 0) + s * PAD
            hot_ref[k, s * PAD:(s + 1) * PAD, :] = jnp.where(index == cell, 1.0, 0.0).astype(BF)
        return carry

    lax.fori_loop(0, 2, make_hot, 0)
    for copy in swap:
        copy.wait()

    left = gy == 0
    own_t = ens_ref[pl.ds(gy * half, half)]
    for lev in range(levels):
        pairs = (
            (own_t[:, lev], o_ens[:, lev], slice(0, half)),
            (wind_ref[:, lev], o_wind[:, lev], slice(half, half + 2)),
        )
        for mine, theirs, where in pairs:
            ext_ref[where, lev, 2:2 + cx, 0:cy] = jnp.where(left, mine, theirs)
            ext_ref[where, lev, 2:2 + cx, cy:2 * cy] = jnp.where(left, theirs, mine)
    for sent, received in halo:
        sent.wait_send()
        received.wait_recv()

    for lev in range(levels):
        for c in range(ny):
            lanes = slice(c * cy, (c + 1) * cy)
            ext_ref[:, lev, 0:2, lanes] = low_ref[c, :, 2 * lev:2 * lev + 2, :]
            ext_ref[:, lev, 2 + cx:4 + cx, lanes] = high_ref[c, :, 2 * lev:2 * lev + 2, :]
    for lev in range(levels):
        east_wind = ext_ref[half, lev][None]
        north_wind = ext_ref[half + 1, lev][None]
        q = ext_ref[0:half, lev]
        for _ in range(STEPS):
            west = pltpu.roll(q, 1, 1)
            east = pltpu.roll(q, cx + 3, 1)
            south = pltpu.roll(q, 1, 2)
            north = pltpu.roll(q, 2 * cy - 1, 2)
            q = (
                q
                - jnp.maximum(east_wind, 0.0) * (q - west)
                - jnp.minimum(east_wind, 0.0) * (east - q)
                - jnp.maximum(north_wind, 0.0) * (q - south)
                - jnp.minimum(north_wind, 0.0) * (north - q)
                + KAPPA * (east + west + north + south - 4.0 * q)
            )
        for c in range(ny):
            piece_ref[c, :, lev * cx:(lev + 1) * cx, :] = q[:, 2:2 + cx, c * cy:(c + 1) * cy]

    own_part = ma * ny + gy
    plane_copies = []
    for i, (m, c) in enumerate(plane):
        source = m * ny + c
        copy = remote(
            piece_ref.at[c], all_ref.at[pl.ds(own_part * half, half)],
            plane_send.at[i], plane_recv.at[own_part], (gx, c, m),
        )
        copy.start()
        plane_copies.append((copy, remote(
            piece_ref.at[gy], all_ref.at[pl.ds(source * half, half)],
            plane_send.at[i], plane_recv.at[source], (gx, c, m),
        )))
    all_ref[pl.ds(own_part * half, half)] = piece_ref[gy]
    lax.fori_loop(2, blocks, make_hot, 0)
    for sent, received in plane_copies:
        sent.wait_send()
        received.wait_recv()

    for s in range(rows):
        lanes = slice(s * cy, (s + 1) * cy)
        values = all_ref[:, s, :]
        flat_ref[:, lanes] = values
        high, low = split(values)
        split_ref[0:members, lanes] = high
        split_ref[members:2 * members, lanes] = low

    def pick(k):
        both = jnp.dot(split_ref[...], hot_ref[k], preferred_element_type=F32)
        base_ref[...] = both[:members] + both[members:]
        part_ref[...] = both.astype(BF)

    def stack(high, low):
        return jnp.concatenate([high, low, high], axis=0)

    def apply(change, stacked):
        high = change.astype(BF).astype(F32)
        blank = jnp.zeros_like(change)
        high, low = (jnp.concatenate([part, blank], axis=1) for part in (high, change - high))
        wide = high + pltpu.roll(high, members, 1) + pltpu.roll(low, 2 * members, 1)
        return jnp.dot(wide.astype(BF)[:, :3 * members], stacked, preferred_element_type=F32)

    def own_rows(x):
        own = x[0:members_dev]
        for m in range(1, nm):
            own = jnp.where(ma == m, x[m * members_dev:(m + 1) * members_dev], own)
        filler = jnp.zeros((-members_dev % 16, x.shape[1]), F32)
        return jnp.concatenate([own, filler], axis=0)

    width = 4 if nx % 4 == 0 else nx
    lane = lax.broadcasted_iota(jnp.int32, (members, PAD), 1)
    top_lane = lane[:mid]
    denom = members - 1.0
    pick(0)
    prior_ref[...] = base_ref[...]
    for sent, received in loc_copies:
        sent.wait_send()
        received.wait_recv()

    mixing_ref[...] = jnp.zeros_like(mixing_ref)
    change_ref[...] = jnp.zeros_like(change_ref)

    def assimilate(k, carry):
        slot = lax.rem(k, 2)
        b = order_ref[k]
        prior = prior_ref[...]
        error_var = var_ref[pl.ds(b, 1), :]
        obs_mean = jnp.sum(prior, axis=0, keepdims=True) / members
        anomaly = prior - obs_mean
        variance = jnp.sum(anomaly * anomaly, axis=0, keepdims=True) / denom
        total_var = variance + error_var
        innovation = value_ref[pl.ds(b, 1), :] - obs_mean
        shrink = 1.0 / (1.0 + jnp.sqrt(error_var / total_var))
        scaled = 1.0 / (denom * total_var)
        lift = innovation * (1.0 + jnp.sqrt(error_var / total_var))
        spread_gain = shrink * scaled
        a_high, a_low = split(anomaly)
        anom_ref[0:members, :] = a_high
        anom_ref[PAD:PAD + members, :] = a_low
        lift_high, lift_low = split(jnp.concatenate([lift, jnp.zeros((15, obs), F32)], axis=0))
        anom_ref[members:members + 16, :] = lift_high
        anom_ref[PAD + members:PAD + members + 16, :] = lift_low

        def line_copy(x, place):
            return remote(
                send_ref.at[slot, gy, x], line_ref.at[slot, place],
                line_send.at[slot, x], line_recv.at[slot, place], (x, gy, ma),
            )

        def group(c, turn, g):
            for j in range(width):
                taper = loc_all[(g * width + j) * ny + c, pl.ds(b, 1), :]
                w_high, w_low = split(anomaly * (taper * spread_gain))
                lhs_ref[turn, 2 * j * members:(2 * j + 1) * members, :] = w_high
                lhs_ref[turn, (2 * j + 1) * members:(2 * j + 2) * members, :] = w_low
            product = lax.dot_general(
                lhs_ref[turn], anom_ref[...], (((1,), (1,)), ((), ())), preferred_element_type=F32
            )
            for j in range(width):
                first = product[2 * j * members:(2 * j + 1) * members]
                second = product[(2 * j + 1) * members:(2 * j + 2) * members, :PAD]
                spread = first[:, :PAD] + first[:, PAD:] + second
                packed = jnp.where(top_lane < members, spread[:mid], pltpu.roll(spread[mid:], mid, 1))
                last = members + mid + 1
                send_ref[slot, c, g * width + j] = jnp.where(
                    top_lane == last, pltpu.roll(spread[:mid], mid + 1, 1), packed
                )

        def contribute(c, turn):
            if nx == width:
                group(c, turn, 0)
            else:
                lax.fori_loop(0, nx // width, lambda g, carry: (group(c, turn, g), carry)[1], 0)

        contribute(other, 0)
        pair = remote(
            send_ref.at[slot, other], pair_ref.at[slot], pair_sem.at[slot, 0], pair_sem.at[slot, 1], (gx, other, ma)
        )
        pair.start()
        contribute(gy, 1)
        pair.wait()
        ahead = [lax.rem(gx + d, nx) for d in range(nx)]
        for x in ahead[1:]:
            send_ref[slot, gy, x] = send_ref[slot, gy, x] + pair_ref[slot, x]
            line_copy(x, gx).start()
        line_ref[slot, gx] = send_ref[slot, gy, gx] + pair_ref[slot, gx]

        @pl.when(k + 1 < blocks)
        def _():
            pick(k + 1)

        @pl.when(k + 1 == blocks)
        def _():
            base_ref[...] = flat_ref[...]
            part_ref[...] = split_ref[...]

        mixing, change = mixing_ref[...], change_ref[...]
        change = change + mixing + apply(mixing, stack(*split(change)))
        change_ref[...] = change
        base = base_ref[...] + apply(change, stack(part_ref[0:members, :], part_ref[members:2 * members, :]))
        base_ref[...] = base
        next_ref[...] = stack(*split(base))

        for x in ahead[1:]:
            line_copy(x, gx).wait_send()
            line_copy(x, x).wait_recv()
        top = line_ref[slot, 0]
        for x in range(1, nx):
            top = top + line_ref[slot, x]
        turned = jnp.concatenate([top, jnp.zeros((PAD - mid, PAD), F32)], axis=0).T
        bottom = jnp.where(top_lane < mid, turned[mid:members], pltpu.roll(top, PAD - mid, 1))
        last = members + mid
        shift = turned[last + 1:last + 2] + pltpu.roll(turned[last:last + 8], mid, 1)[0:1]
        mixing = shift - jnp.concatenate([top, bottom], axis=0)
        mixing = jnp.where(lane < members, mixing, 0.0)
        centre = jnp.sum(mixing, axis=1, keepdims=True) / members
        mixing = jnp.where(lane < members, mixing - centre, 0.0)
        mixing_ref[...] = mixing

        @pl.when(k + 1 < blocks)
        def _():
            prior_ref[...] = base + apply(mixing, next_ref[...])

        return carry

    lax.fori_loop(0, blocks, assimilate, 0)
    base, mixing = own_rows(base_ref[...]), mixing_ref[...]
    mine = base + apply(own_rows(mixing), next_ref[...])
    for lev in range(levels):
        for x in range(cx):
            s = lev * cx + x
            out_ref[:, lev, x, :] = mine[0:members_dev, s * cy:(s + 1) * cy]


def local(
    ensemble, wind_field, obs_value, obs_var, obs_region, obs_cell, block_order, localization
):
    nx, ny, nm = lax.axis_size("gx"), lax.axis_size("gy"), lax.axis_size("ma")
    members_dev, levels, cx, cy = ensemble.shape
    half = members_dev // 2
    members = members_dev * nm
    blocks, obs = obs_value.shape
    rows = levels * cx
    cells = rows * cy
    regions = nx * ny
    width = 4 if nx % 4 == 0 else nx
    dma = pltpu.SemaphoreType.DMA
    vmem = pl.BlockSpec(memory_space=pltpu.VMEM)
    return pl.pallas_call(
        functools.partial(kernel, nx, ny, nm),
        out_shape=jax.ShapeDtypeStruct(ensemble.shape, F32),
        in_specs=[pl.BlockSpec(memory_space=pltpu.SMEM)] + [pl.BlockSpec(memory_space=pl.ANY)] * 7,
        out_specs=vmem,
        scratch_shapes=[
            pltpu.VMEM(ensemble.shape, F32),
            pltpu.VMEM(wind_field.shape, F32),
            pltpu.VMEM(obs_value.shape, F32),
            pltpu.VMEM(obs_var.shape, F32),
            pltpu.VMEM(obs_region.shape, jnp.int32),
            pltpu.VMEM(obs_cell.shape, jnp.int32),
            pltpu.VMEM(localization.shape, F32),
            dma((7,)),
            pltpu.VMEM((half, levels, cx, cy), F32),
            pltpu.VMEM(wind_field.shape, F32),
            pltpu.VMEM((ny, half + 2, 2 * levels, cy), F32),
            pltpu.VMEM((ny, half + 2, 2 * levels, cy), F32),
            pltpu.VMEM((ny, half + 2, 2 * levels, cy), F32),
            pltpu.VMEM((ny, half + 2, 2 * levels, cy), F32),
            pltpu.VMEM((half + 2, levels, cx + 4, 2 * cy), F32),
            pltpu.VMEM((ny, half, rows, cy), F32),
            pltpu.VMEM((members, rows, cy), F32),
            pltpu.VMEM((members, cells), F32),
            pltpu.VMEM((2 * members, cells), BF),
            pltpu.VMEM((regions, blocks, obs), F32),
            pltpu.VMEM((blocks, cells, obs), BF),
            pltpu.VMEM((2, 2 * width * members, obs), BF),
            pltpu.VMEM((3 * members, cells), BF),
            pltpu.VMEM((2 * PAD, obs), BF),
            pltpu.VMEM((2, ny, nx, members // 2, PAD), F32),
            pltpu.VMEM((2, nx, members // 2, PAD), F32),
            pltpu.VMEM((2, nx, members // 2, PAD), F32),
            pltpu.VMEM((members, obs), F32),
            pltpu.VMEM((2 * members, obs), BF),
            pltpu.VMEM((members, obs), F32),
            pltpu.VMEM((members, PAD), F32),
            pltpu.VMEM((members, PAD), F32),
            dma((4,)),
            dma((2, ny)),
            dma((2, ny)),
            dma((regions,)),
            dma((regions,)),
            dma((nm * ny,)),
            dma((nm * ny,)),
            dma((2, 2)),
            dma((2, nx)),
            dma((2, nx)),
        ],
        compiler_params=pltpu.CompilerParams(
            collective_id=0, has_side_effects=True, vmem_limit_bytes=56 * 1024 * 1024
        ),
    )(block_order, ensemble, wind_field, obs_value, obs_var, obs_region, obs_cell, localization)


def solution(mesh):
    in_specs = (
        P("ma", None, "gx", "gy"),
        P(None, None, "gx", "gy"),
        P(),
        P(),
        P(),
        P(),
        P(),
        P("gx", "gy", None, None),
    )
    out_specs = P("ma", None, "gx", "gy")
    return jax.shard_map(local, mesh=mesh, in_specs=in_specs, out_specs=out_specs, check_vma=False)
```

```python
import functools

import jax
import jax.numpy as jnp
from jax import lax
from jax.experimental import pallas as pl
from jax.experimental.pallas import tpu as pltpu
from jax.sharding import PartitionSpec as P

STEPS = 2
KAPPA = 0.025
PAD = 128
MESH = pl.DeviceIdType.MESH
BF = jnp.bfloat16
F32 = jnp.float32


def split(x):
    high = x.astype(BF)
    return high, (x - high.astype(F32)).astype(BF)


def kernel(
    nx, ny, nm,
    order_ref, ens_in, wind_in, value_in, var_in, region_in, cell_in, loc_in,
    out_ref,
    ens_ref, wind_ref, value_ref, var_ref, region_ref, cell_ref, loc_ref, in_sem,
    o_ens, o_wind, up_ref, down_ref, low_ref, high_ref, ext_ref, piece_ref,
    all_ref, flat_ref, split_ref, loc_all, hot_ref, quarter_ref, lhs_ref, next_ref, anom_ref,
    send_ref, pair_ref, line_ref, base_ref, part_ref, prior_ref, mixing_ref, change_ref,
    swap_sem, halo_send, halo_recv, loc_send, loc_recv, plane_send, plane_recv,
    pair_sem, line_send, line_recv,
):
    members_dev, levels, cx, cy = ens_ref.shape
    half = members_dev // 2
    members = members_dev * nm
    mid = members // 2
    blocks, obs = value_ref.shape
    cells = levels * cx * cy
    rows = levels * cx
    quarters = cells // (2 * PAD)
    gx, gy, ma = lax.axis_index("gx"), lax.axis_index("gy"), lax.axis_index("ma")
    other = 1 - gy

    def remote(src, dst, send_sem, recv_sem, device):
        return pltpu.make_async_remote_copy(
            src_ref=src, dst_ref=dst, send_sem=send_sem, recv_sem=recv_sem,
            device_id=device, device_id_type=MESH,
        )

    line = [(lax.rem(gx + d, nx), c) for d in range(nx) for c in range(ny) if d or c]
    line = [(x, lax.rem(gy + c, ny)) for x, c in line]
    plane = [(lax.rem(ma + d, nm), lax.rem(gy + c, ny)) for d in range(nm) for c in range(ny) if d or c]

    barrier = pltpu.get_barrier_semaphore()
    for x, c in line:
        pl.semaphore_signal(barrier, inc=1, device_id=(x, c, ma), device_id_type=MESH)
    for m, c in plane[ny - 1:]:
        pl.semaphore_signal(barrier, inc=1, device_id=(gx, c, m), device_id_type=MESH)

    inputs = [
        pltpu.make_async_copy(src, dst, in_sem.at[i])
        for i, (src, dst) in enumerate((
            (ens_in, ens_ref), (wind_in, wind_ref), (region_in, region_ref), (cell_in, cell_ref),
            (loc_in, loc_ref), (value_in, value_ref), (var_in, var_ref),
        ))
    ]
    for copy in inputs:
        copy.start()
    for copy in inputs[:2]:
        copy.wait()

    for c in range(ny):
        for lev in range(levels):
            pair_rows = slice(2 * lev, 2 * lev + 2)
            part = ens_ref[c * half:(c + 1) * half, lev]
            winds = wind_ref[:, lev]
            up_ref[c, 0:half, pair_rows, :] = part[:, cx - 2:cx]
            up_ref[c, half:half + 2, pair_rows, :] = winds[:, cx - 2:cx]
            down_ref[c, 0:half, pair_rows, :] = part[:, 0:2]
            down_ref[c, half:half + 2, pair_rows, :] = winds[:, 0:2]
    anom_ref[...] = jnp.zeros_like(anom_ref)

    for copy in inputs[2:]:
        copy.wait()
    pl.semaphore_wait(barrier, len(line) + len(plane) - (ny - 1))

    after, before = lax.rem(gx + 1, nx), lax.rem(gx + nx - 1, nx)
    halo = []
    for c in range(ny):
        for way, (src, dst, to, source) in enumerate(
            ((up_ref, low_ref, after, before), (down_ref, high_ref, before, after))
        ):
            copy = remote(src.at[c], dst.at[gy], halo_send.at[way, c], halo_recv.at[way, gy], (to, c, ma))
            copy.start()
            halo.append((copy, remote(
                src.at[c], dst.at[c], halo_send.at[way, c], halo_recv.at[way, c], (source, c, ma)
            )))
    swap = [
        remote(ens_ref.at[pl.ds(other * half, half)], o_ens, swap_sem.at[0], swap_sem.at[1], (gx, other, ma)),
        remote(wind_ref, o_wind, swap_sem.at[2], swap_sem.at[3], (gx, other, ma)),
    ]
    for copy in swap:
        copy.start()

    own_region = gx * ny + gy
    loc_copies = []
    for i, (x, c) in enumerate(line):
        source = x * ny + c
        copy = remote(loc_ref.at[0, 0], loc_all.at[own_region], loc_send.at[i], loc_recv.at[own_region], (x, c, ma))
        copy.start()
        loc_copies.append((copy, remote(loc_ref.at[0, 0], loc_all.at[source], loc_send.at[i], loc_recv.at[source], (x, c, ma))))
    loc_all[own_region] = loc_ref[0, 0]

    def make_hot(k, carry):
        b = order_ref[k]
        cell = jnp.where(region_ref[pl.ds(b, 1), :] == own_region, cell_ref[pl.ds(b, 1), :], -1)
        quarter = lax.shift_right_arithmetic(cell, 8)
        quarter_ref[k] = quarter
        place = jnp.where(cell < 0, -1, cell - quarter * (2 * PAD))
        for s in range(2):
            index = lax.broadcasted_iota(jnp.int32, (PAD, obs), 0) + s * PAD
            hot_ref[k, s * PAD:(s + 1) * PAD, :] = jnp.where(index == place, 1.0, 0.0).astype(BF)
        return carry

    lax.fori_loop(0, 2, make_hot, 0)
    for copy in swap:
        copy.wait()

    left = gy == 0
    own_t = ens_ref[pl.ds(gy * half, half)]
    for lev in range(levels):
        pairs = (
            (own_t[:, lev], o_ens[:, lev], slice(0, half)),
            (wind_ref[:, lev], o_wind[:, lev], slice(half, half + 2)),
        )
        for mine, theirs, where in pairs:
            ext_ref[where, lev, 2:2 + cx, 0:cy] = jnp.where(left, mine, theirs)
            ext_ref[where, lev, 2:2 + cx, cy:2 * cy] = jnp.where(left, theirs, mine)
    for sent, received in halo:
        sent.wait_send()
        received.wait_recv()

    for lev in range(levels):
        for c in range(ny):
            lanes = slice(c * cy, (c + 1) * cy)
            ext_ref[:, lev, 0:2, lanes] = low_ref[c, :, 2 * lev:2 * lev + 2, :]
            ext_ref[:, lev, 2 + cx:4 + cx, lanes] = high_ref[c, :, 2 * lev:2 * lev + 2, :]
    for lev in range(levels):
        east_wind = ext_ref[half, lev][None]
        north_wind = ext_ref[half + 1, lev][None]
        q = ext_ref[0:half, lev]
        for _ in range(STEPS):
            west = pltpu.roll(q, 1, 1)
            east = pltpu.roll(q, cx + 3, 1)
            south = pltpu.roll(q, 1, 2)
            north = pltpu.roll(q, 2 * cy - 1, 2)
            q = (
                q
                - jnp.maximum(east_wind, 0.0) * (q - west)
                - jnp.minimum(east_wind, 0.0) * (east - q)
                - jnp.maximum(north_wind, 0.0) * (q - south)
                - jnp.minimum(north_wind, 0.0) * (north - q)
                + KAPPA * (east + west + north + south - 4.0 * q)
            )
        for c in range(ny):
            piece_ref[c, :, lev * cx:(lev + 1) * cx, :] = q[:, 2:2 + cx, c * cy:(c + 1) * cy]

    own_part = ma * ny + gy
    plane_copies = []
    for i, (m, c) in enumerate(plane):
        source = m * ny + c
        copy = remote(
            piece_ref.at[c], all_ref.at[pl.ds(own_part * half, half)],
            plane_send.at[i], plane_recv.at[own_part], (gx, c, m),
        )
        copy.start()
        plane_copies.append((copy, remote(
            piece_ref.at[gy], all_ref.at[pl.ds(source * half, half)],
            plane_send.at[i], plane_recv.at[source], (gx, c, m),
        )))
    all_ref[pl.ds(own_part * half, half)] = piece_ref[gy]
    lax.fori_loop(2, blocks, make_hot, 0)
    for sent, received in plane_copies:
        sent.wait_send()
        received.wait_recv()

    for s in range(rows):
        lanes = slice(s * cy, (s + 1) * cy)
        values = all_ref[:, s, :]
        flat_ref[:, lanes] = values
        high, low = split(values)
        within = slice(s % 2 * cy, (s % 2 + 1) * cy)
        split_ref[s // 2, 0:members, within] = high
        split_ref[s // 2, members:2 * members, within] = low

    def pick(k):
        quarter = quarter_ref[k]
        lhs = split_ref[...].reshape(quarters * 2 * members, 2 * PAD)
        product = jnp.dot(lhs, hot_ref[k], preferred_element_type=F32)
        both = product[:2 * members]
        for q in range(1, quarters):
            both = jnp.where(quarter == q, product[2 * q * members:2 * (q + 1) * members], both)
        base_ref[...] = both[:members] + both[members:]
        part_ref[...] = both.astype(BF)

    def stack(high, low):
        return jnp.concatenate([high, low, high], axis=0)

    def apply(change, stacked):
        high = change.astype(BF).astype(F32)
        blank = jnp.zeros_like(change)
        high, low = (jnp.concatenate([part, blank], axis=1) for part in (high, change - high))
        wide = high + pltpu.roll(high, members, 1) + pltpu.roll(low, 2 * members, 1)
        return jnp.dot(wide.astype(BF)[:, :3 * members], stacked, preferred_element_type=F32)

    def own_rows(x):
        own = x[0:members_dev]
        for m in range(1, nm):
            own = jnp.where(ma == m, x[m * members_dev:(m + 1) * members_dev], own)
        filler = jnp.zeros((-members_dev % 16, x.shape[1]), F32)
        return jnp.concatenate([own, filler], axis=0)

    width = 4 if nx % 4 == 0 else nx
    lane = lax.broadcasted_iota(jnp.int32, (members, PAD), 1)
    top_lane = lane[:mid]
    denom = members - 1.0
    pick(0)
    prior_ref[...] = base_ref[...]
    for sent, received in loc_copies:
        sent.wait_send()
        received.wait_recv()

    def assimilate(k, carry):
        slot = lax.rem(k, 2)
        b = order_ref[k]
        prior = prior_ref[...]
        error_var = var_ref[pl.ds(b, 1), :]
        obs_mean = jnp.sum(prior, axis=0, keepdims=True) / members
        anomaly = prior - obs_mean
        variance = jnp.sum(anomaly * anomaly, axis=0, keepdims=True) / denom
        total_var = variance + error_var
        innovation = value_ref[pl.ds(b, 1), :] - obs_mean
        shrink = 1.0 / (1.0 + jnp.sqrt(error_var / total_var))
        scaled = 1.0 / (denom * total_var)
        lift = innovation * (1.0 + jnp.sqrt(error_var / total_var))
        spread_gain = shrink * scaled
        a_high, a_low = split(anomaly)
        anom_ref[0:members, :] = a_high
        anom_ref[PAD:PAD + members, :] = a_low
        lift_high, lift_low = split(jnp.concatenate([lift, jnp.zeros((15, obs), F32)], axis=0))
        anom_ref[members:members + 16, :] = lift_high
        anom_ref[PAD + members:PAD + members + 16, :] = lift_low

        def line_copy(x, place):
            return remote(
                send_ref.at[slot, gy, x], line_ref.at[slot, place],
                line_send.at[slot, x], line_recv.at[slot, place], (x, gy, ma),
            )

        def group(c, turn, g):
            for j in range(width):
                taper = loc_all[(g * width + j) * ny + c, pl.ds(b, 1), :]
                w_high, w_low = split(anomaly * (taper * spread_gain))
                lhs_ref[turn, 2 * j * members:(2 * j + 1) * members, :] = w_high
                lhs_ref[turn, (2 * j + 1) * members:(2 * j + 2) * members, :] = w_low
            product = lax.dot_general(
                lhs_ref[turn], anom_ref[...], (((1,), (1,)), ((), ())), preferred_element_type=F32
            )
            for j in range(width):
                first = product[2 * j * members:(2 * j + 1) * members]
                second = product[(2 * j + 1) * members:(2 * j + 2) * members, :PAD]
                spread = first[:, :PAD] + first[:, PAD:] + second
                packed = jnp.where(top_lane < members, spread[:mid], pltpu.roll(spread[mid:], mid, 1))
                last = members + mid + 1
                send_ref[slot, c, g * width + j] = jnp.where(
                    top_lane == last, pltpu.roll(spread[:mid], mid + 1, 1), packed
                )

        def contribute(c, turn):
            if nx == width:
                group(c, turn, 0)
            else:
                lax.fori_loop(0, nx // width, lambda g, carry: (group(c, turn, g), carry)[1], 0)

        contribute(other, 0)
        pair = remote(
            send_ref.at[slot, other], pair_ref.at[slot], pair_sem.at[slot, 0], pair_sem.at[slot, 1], (gx, other, ma)
        )
        pair.start()
        contribute(gy, 1)
        pair.wait()
        ahead = [lax.rem(gx + d, nx) for d in range(nx)]
        for x in ahead[1:]:
            send_ref[slot, gy, x] = send_ref[slot, gy, x] + pair_ref[slot, x]
            line_copy(x, gx).start()
        line_ref[slot, gx] = send_ref[slot, gy, gx] + pair_ref[slot, gx]

        @pl.when(k + 1 < blocks)
        def _():
            pick(k + 1)

        @pl.when(k + 1 == blocks)
        def _():
            base_ref[...] = flat_ref[...]
            for q in range(quarters):
                part_ref[:, 2 * q * PAD:2 * (q + 1) * PAD] = split_ref[q]

        @pl.when(k == 1)
        def _():
            change_ref[...] = mixing_ref[...]

        @pl.when(k > 1)
        def _():
            mixing, change = mixing_ref[...], change_ref[...]
            change_ref[...] = change + mixing + apply(mixing, stack(*split(change)))

        @pl.when(k > 0)
        def _():
            stacked = stack(part_ref[0:members, :], part_ref[members:2 * members, :])
            base = base_ref[...] + apply(change_ref[...], stacked)
            base_ref[...] = base
            high, low = split(base)
            part_ref[0:members, :] = high
            part_ref[members:2 * members, :] = low

        next_ref[...] = stack(part_ref[0:members, :], part_ref[members:2 * members, :])

        for x in ahead[1:]:
            line_copy(x, gx).wait_send()
            line_copy(x, x).wait_recv()
        top = line_ref[slot, 0]
        for x in range(1, nx):
            top = top + line_ref[slot, x]
        turned = jnp.concatenate([top, jnp.zeros((PAD - mid, PAD), F32)], axis=0).T
        bottom = jnp.where(top_lane < mid, turned[mid:members], pltpu.roll(top, PAD - mid, 1))
        last = members + mid
        shift = turned[last + 1:last + 2] + pltpu.roll(turned[last:last + 8], mid, 1)[0:1]
        mixing = shift - jnp.concatenate([top, bottom], axis=0)
        mixing = jnp.where(lane < members, mixing, 0.0)
        centre = jnp.sum(mixing, axis=1, keepdims=True) / members
        mixing = jnp.where(lane < members, mixing - centre, 0.0)
        mixing_ref[...] = mixing

        @pl.when(k + 1 < blocks)
        def _():
            prior_ref[...] = base_ref[...] + apply(mixing, next_ref[...])

        return carry

    lax.fori_loop(0, blocks, assimilate, 0)
    base, mixing = own_rows(base_ref[...]), mixing_ref[...]
    mine = base + apply(own_rows(mixing), next_ref[...])
    for lev in range(levels):
        for x in range(cx):
            s = lev * cx + x
            out_ref[:, lev, x, :] = mine[0:members_dev, s * cy:(s + 1) * cy]


def local(
    ensemble, wind_field, obs_value, obs_var, obs_region, obs_cell, block_order, localization
):
    nx, ny, nm = lax.axis_size("gx"), lax.axis_size("gy"), lax.axis_size("ma")
    members_dev, levels, cx, cy = ensemble.shape
    half = members_dev // 2
    members = members_dev * nm
    blocks, obs = obs_value.shape
    rows = levels * cx
    cells = rows * cy
    regions = nx * ny
    width = 4 if nx % 4 == 0 else nx
    dma = pltpu.SemaphoreType.DMA
    vmem = pl.BlockSpec(memory_space=pltpu.VMEM)
    return pl.pallas_call(
        functools.partial(kernel, nx, ny, nm),
        out_shape=jax.ShapeDtypeStruct(ensemble.shape, F32),
        in_specs=[pl.BlockSpec(memory_space=pltpu.SMEM)] + [pl.BlockSpec(memory_space=pl.ANY)] * 7,
        out_specs=vmem,
        scratch_shapes=[
            pltpu.VMEM(ensemble.shape, F32),
            pltpu.VMEM(wind_field.shape, F32),
            pltpu.VMEM(obs_value.shape, F32),
            pltpu.VMEM(obs_var.shape, F32),
            pltpu.VMEM(obs_region.shape, jnp.int32),
            pltpu.VMEM(obs_cell.shape, jnp.int32),
            pltpu.VMEM(localization.shape, F32),
            dma((7,)),
            pltpu.VMEM((half, levels, cx, cy), F32),
            pltpu.VMEM(wind_field.shape, F32),
            pltpu.VMEM((ny, half + 2, 2 * levels, cy), F32),
            pltpu.VMEM((ny, half + 2, 2 * levels, cy), F32),
            pltpu.VMEM((ny, half + 2, 2 * levels, cy), F32),
            pltpu.VMEM((ny, half + 2, 2 * levels, cy), F32),
            pltpu.VMEM((half + 2, levels, cx + 4, 2 * cy), F32),
            pltpu.VMEM((ny, half, rows, cy), F32),
            pltpu.VMEM((members, rows, cy), F32),
            pltpu.VMEM((members, cells), F32),
            pltpu.VMEM((cells // (2 * PAD), 2 * members, 2 * PAD), BF),
            pltpu.VMEM((regions, blocks, obs), F32),
            pltpu.VMEM((blocks, 2 * PAD, obs), BF),
            pltpu.VMEM((blocks, 1, obs), jnp.int32),
            pltpu.VMEM((2, 2 * width * members, obs), BF),
            pltpu.VMEM((3 * members, cells), BF),
            pltpu.VMEM((2 * PAD, obs), BF),
            pltpu.VMEM((2, ny, nx, members // 2, PAD), F32),
            pltpu.VMEM((2, nx, members // 2, PAD), F32),
            pltpu.VMEM((2, nx, members // 2, PAD), F32),
            pltpu.VMEM((members, obs), F32),
            pltpu.VMEM((2 * members, obs), BF),
            pltpu.VMEM((members, obs), F32),
            pltpu.VMEM((members, PAD), F32),
            pltpu.VMEM((members, PAD), F32),
            dma((4,)),
            dma((2, ny)),
            dma((2, ny)),
            dma((regions,)),
            dma((regions,)),
            dma((nm * ny,)),
            dma((nm * ny,)),
            dma((2, 2)),
            dma((2, nx)),
            dma((2, nx)),
        ],
        compiler_params=pltpu.CompilerParams(
            collective_id=0, has_side_effects=True, vmem_limit_bytes=56 * 1024 * 1024
        ),
    )(block_order, ensemble, wind_field, obs_value, obs_var, obs_region, obs_cell, localization)


def solution(mesh):
    in_specs = (
        P("ma", None, "gx", "gy"),
        P(None, None, "gx", "gy"),
        P(),
        P(),
        P(),
        P(),
        P(),
        P("gx", "gy", None, None),
    )
    out_specs = P("ma", None, "gx", "gy")
    return jax.shard_map(local, mesh=mesh, in_specs=in_specs, out_specs=out_specs, check_vma=False)
```

```python
import functools

import jax
import jax.numpy as jnp
from jax import lax
from jax.experimental import pallas as pl
from jax.experimental.pallas import tpu as pltpu
from jax.sharding import PartitionSpec as P

STEPS = 2
KAPPA = 0.025
PAD = 128
MESH = pl.DeviceIdType.MESH
BF = jnp.bfloat16
F32 = jnp.float32


def split(x):
    high = x.astype(BF)
    return high, (x - high.astype(F32)).astype(BF)


def kernel(
    nx, ny, nm,
    order_ref, ens_in, wind_in, value_in, var_in, region_in, cell_in, loc_in,
    out_ref,
    ens_ref, wind_ref, value_ref, var_ref, region_ref, cell_ref, loc_ref, in_sem,
    o_ens, o_wind, up_ref, down_ref, low_ref, high_ref, ext_ref, piece_ref,
    all_ref, flat_ref, split_ref, loc_all, hot_ref, quarter_ref, lhs_ref, next_ref, anom_ref, turned_ref,
    send_ref, pair_ref, line_ref, base_ref, part_ref, prior_ref, mixing_ref, change_ref,
    swap_sem, halo_send, halo_recv, loc_send, loc_recv, plane_send, plane_recv,
    pair_sem, line_send, line_recv,
):
    members_dev, levels, cx, cy = ens_ref.shape
    half = members_dev // 2
    members = members_dev * nm
    mid = members // 2
    blocks, obs = value_ref.shape
    cells = levels * cx * cy
    rows = levels * cx
    quarters = cells // (2 * PAD)
    gx, gy, ma = lax.axis_index("gx"), lax.axis_index("gy"), lax.axis_index("ma")
    other = 1 - gy

    def remote(src, dst, send_sem, recv_sem, device):
        return pltpu.make_async_remote_copy(
            src_ref=src, dst_ref=dst, send_sem=send_sem, recv_sem=recv_sem,
            device_id=device, device_id_type=MESH,
        )

    line = [(lax.rem(gx + d, nx), c) for d in range(nx) for c in range(ny) if d or c]
    line = [(x, lax.rem(gy + c, ny)) for x, c in line]
    plane = [(lax.rem(ma + d, nm), lax.rem(gy + c, ny)) for d in range(nm) for c in range(ny) if d or c]

    barrier = pltpu.get_barrier_semaphore()
    for x, c in line:
        pl.semaphore_signal(barrier, inc=1, device_id=(x, c, ma), device_id_type=MESH)
    for m, c in plane[ny - 1:]:
        pl.semaphore_signal(barrier, inc=1, device_id=(gx, c, m), device_id_type=MESH)

    inputs = [
        pltpu.make_async_copy(src, dst, in_sem.at[i])
        for i, (src, dst) in enumerate((
            (ens_in, ens_ref), (wind_in, wind_ref), (region_in, region_ref), (cell_in, cell_ref),
            (loc_in, loc_ref), (value_in, value_ref), (var_in, var_ref),
        ))
    ]
    for copy in inputs:
        copy.start()
    for copy in inputs[:2]:
        copy.wait()

    for c in range(ny):
        for lev in range(levels):
            pair_rows = slice(2 * lev, 2 * lev + 2)
            part = ens_ref[c * half:(c + 1) * half, lev]
            winds = wind_ref[:, lev]
            up_ref[c, 0:half, pair_rows, :] = part[:, cx - 2:cx]
            up_ref[c, half:half + 2, pair_rows, :] = winds[:, cx - 2:cx]
            down_ref[c, 0:half, pair_rows, :] = part[:, 0:2]
            down_ref[c, half:half + 2, pair_rows, :] = winds[:, 0:2]
    anom_ref[...] = jnp.zeros_like(anom_ref)

    for copy in inputs[2:]:
        copy.wait()
    pl.semaphore_wait(barrier, len(line) + len(plane) - (ny - 1))

    after, before = lax.rem(gx + 1, nx), lax.rem(gx + nx - 1, nx)
    halo = []
    for c in range(ny):
        for way, (src, dst, to, source) in enumerate(
            ((up_ref, low_ref, after, before), (down_ref, high_ref, before, after))
        ):
            copy = remote(src.at[c], dst.at[gy], halo_send.at[way, c], halo_recv.at[way, gy], (to, c, ma))
            copy.start()
            halo.append((copy, remote(
                src.at[c], dst.at[c], halo_send.at[way, c], halo_recv.at[way, c], (source, c, ma)
            )))
    swap = [
        remote(ens_ref.at[pl.ds(other * half, half)], o_ens, swap_sem.at[0], swap_sem.at[1], (gx, other, ma)),
        remote(wind_ref, o_wind, swap_sem.at[2], swap_sem.at[3], (gx, other, ma)),
    ]
    for copy in swap:
        copy.start()

    own_region = gx * ny + gy
    loc_copies = []
    for i, (x, c) in enumerate(line):
        source = x * ny + c
        copy = remote(loc_ref.at[0, 0], loc_all.at[own_region], loc_send.at[i], loc_recv.at[own_region], (x, c, ma))
        copy.start()
        loc_copies.append((copy, remote(loc_ref.at[0, 0], loc_all.at[source], loc_send.at[i], loc_recv.at[source], (x, c, ma))))
    loc_all[own_region] = loc_ref[0, 0]

    def make_hot(k, carry):
        b = order_ref[k]
        cell = jnp.where(region_ref[pl.ds(b, 1), :] == own_region, cell_ref[pl.ds(b, 1), :], -1)
        quarter = lax.shift_right_arithmetic(cell, 8)
        quarter_ref[k] = quarter
        place = jnp.where(cell < 0, -1, cell - quarter * (2 * PAD))
        for s in range(2):
            index = lax.broadcasted_iota(jnp.int32, (PAD, obs), 0) + s * PAD
            hot_ref[k, s * PAD:(s + 1) * PAD, :] = jnp.where(index == place, 1.0, 0.0).astype(BF)
        return carry

    lax.fori_loop(0, 2, make_hot, 0)
    for copy in swap:
        copy.wait()

    left = gy == 0
    own_t = ens_ref[pl.ds(gy * half, half)]
    for lev in range(levels):
        pairs = (
            (own_t[:, lev], o_ens[:, lev], slice(0, half)),
            (wind_ref[:, lev], o_wind[:, lev], slice(half, half + 2)),
        )
        for mine, theirs, where in pairs:
            ext_ref[where, lev, 2:2 + cx, 0:cy] = jnp.where(left, mine, theirs)
            ext_ref[where, lev, 2:2 + cx, cy:2 * cy] = jnp.where(left, theirs, mine)
    for sent, received in halo:
        sent.wait_send()
        received.wait_recv()

    for lev in range(levels):
        for c in range(ny):
            lanes = slice(c * cy, (c + 1) * cy)
            ext_ref[:, lev, 0:2, lanes] = low_ref[c, :, 2 * lev:2 * lev + 2, :]
            ext_ref[:, lev, 2 + cx:4 + cx, lanes] = high_ref[c, :, 2 * lev:2 * lev + 2, :]
    for lev in range(levels):
        east_wind = ext_ref[half, lev][None]
        north_wind = ext_ref[half + 1, lev][None]
        q = ext_ref[0:half, lev]
        for _ in range(STEPS):
            west = pltpu.roll(q, 1, 1)
            east = pltpu.roll(q, cx + 3, 1)
            south = pltpu.roll(q, 1, 2)
            north = pltpu.roll(q, 2 * cy - 1, 2)
            q = (
                q
                - jnp.maximum(east_wind, 0.0) * (q - west)
                - jnp.minimum(east_wind, 0.0) * (east - q)
                - jnp.maximum(north_wind, 0.0) * (q - south)
                - jnp.minimum(north_wind, 0.0) * (north - q)
                + KAPPA * (east + west + north + south - 4.0 * q)
            )
        for c in range(ny):
            piece_ref[c, :, lev * cx:(lev + 1) * cx, :] = q[:, 2:2 + cx, c * cy:(c + 1) * cy]

    own_part = ma * ny + gy
    plane_copies = []
    for i, (m, c) in enumerate(plane):
        source = m * ny + c
        copy = remote(
            piece_ref.at[c], all_ref.at[pl.ds(own_part * half, half)],
            plane_send.at[i], plane_recv.at[own_part], (gx, c, m),
        )
        copy.start()
        plane_copies.append((copy, remote(
            piece_ref.at[gy], all_ref.at[pl.ds(source * half, half)],
            plane_send.at[i], plane_recv.at[source], (gx, c, m),
        )))
    all_ref[pl.ds(own_part * half, half)] = piece_ref[gy]
    lax.fori_loop(2, blocks, make_hot, 0)
    for sent, received in plane_copies:
        sent.wait_send()
        received.wait_recv()

    for s in range(rows):
        lanes = slice(s * cy, (s + 1) * cy)
        values = all_ref[:, s, :]
        flat_ref[:, lanes] = values
        high, low = split(values)
        within = slice(s % 2 * cy, (s % 2 + 1) * cy)
        split_ref[s // 2, 0:members, within] = high
        split_ref[s // 2, members:2 * members, within] = low

    def pick(k):
        quarter = quarter_ref[k]
        lhs = split_ref[...].reshape(quarters * 2 * members, 2 * PAD)
        product = jnp.dot(lhs, hot_ref[k], preferred_element_type=F32)
        both = product[:2 * members]
        for q in range(1, quarters):
            both = jnp.where(quarter == q, product[2 * q * members:2 * (q + 1) * members], both)
        base_ref[...] = both[:members] + both[members:]
        part_ref[...] = both.astype(BF)

    def stack(high, low):
        return jnp.concatenate([high, low, high], axis=0)

    def apply(change, stacked):
        high = change.astype(BF).astype(F32)
        blank = jnp.zeros_like(change)
        high, low = (jnp.concatenate([part, blank], axis=1) for part in (high, change - high))
        wide = high + pltpu.roll(high, members, 1) + pltpu.roll(low, 2 * members, 1)
        return jnp.dot(wide.astype(BF)[:, :3 * members], stacked, preferred_element_type=F32)

    def own_rows(x):
        own = x[0:members_dev]
        for m in range(1, nm):
            own = jnp.where(ma == m, x[m * members_dev:(m + 1) * members_dev], own)
        filler = jnp.zeros((-members_dev % 16, x.shape[1]), F32)
        return jnp.concatenate([own, filler], axis=0)

    width = 4 if nx % 4 == 0 else nx
    lane = lax.broadcasted_iota(jnp.int32, (members, PAD), 1)
    top_lane = lane[:mid]
    denom = members - 1.0
    pick(0)
    prior_ref[...] = base_ref[...]
    for sent, received in loc_copies:
        sent.wait_send()
        received.wait_recv()

    def assimilate(k, carry):
        slot = lax.rem(k, 2)
        b = order_ref[k]
        prior = prior_ref[...]
        error_var = var_ref[pl.ds(b, 1), :]
        obs_mean = jnp.sum(prior, axis=0, keepdims=True) / members
        anomaly = prior - obs_mean
        variance = jnp.sum(anomaly * anomaly, axis=0, keepdims=True) / denom
        total_var = variance + error_var
        innovation = value_ref[pl.ds(b, 1), :] - obs_mean
        shrink = 1.0 / (1.0 + jnp.sqrt(error_var / total_var))
        scaled = 1.0 / (denom * total_var)
        lift = innovation * (1.0 + jnp.sqrt(error_var / total_var))
        spread_gain = shrink * scaled
        a_high, a_low = split(anomaly)
        anom_ref[0:members, :] = a_high
        anom_ref[PAD:PAD + members, :] = a_low
        lift_high, lift_low = split(jnp.concatenate([lift, jnp.zeros((15, obs), F32)], axis=0))
        anom_ref[members:members + 16, :] = lift_high
        anom_ref[PAD + members:PAD + members + 16, :] = lift_low

        turned_ref[...] = anom_ref[...].T

        def line_copy(x, place):
            return remote(
                send_ref.at[slot, gy, x], line_ref.at[slot, place],
                line_send.at[slot, x], line_recv.at[slot, place], (x, gy, ma),
            )

        def group(c, turn, g):
            for j in range(width):
                taper = loc_all[(g * width + j) * ny + c, pl.ds(b, 1), :]
                w_high, w_low = split(anomaly * (taper * spread_gain))
                lhs_ref[turn, 2 * j * members:(2 * j + 1) * members, :] = w_high
                lhs_ref[turn, (2 * j + 1) * members:(2 * j + 2) * members, :] = w_low
            product = jnp.dot(lhs_ref[turn], turned_ref[...], preferred_element_type=F32)
            for j in range(width):
                first = product[2 * j * members:(2 * j + 1) * members]
                second = product[(2 * j + 1) * members:(2 * j + 2) * members, :PAD]
                spread = first[:, :PAD] + first[:, PAD:] + second
                packed = jnp.where(top_lane < members, spread[:mid], pltpu.roll(spread[mid:], mid, 1))
                last = members + mid + 1
                send_ref[slot, c, g * width + j] = jnp.where(
                    top_lane == last, pltpu.roll(spread[:mid], mid + 1, 1), packed
                )

        def contribute(c, turn):
            if nx == width:
                group(c, turn, 0)
            else:
                lax.fori_loop(0, nx // width, lambda g, carry: (group(c, turn, g), carry)[1], 0)

        contribute(other, 0)
        pair = remote(
            send_ref.at[slot, other], pair_ref.at[slot], pair_sem.at[slot, 0], pair_sem.at[slot, 1], (gx, other, ma)
        )
        pair.start()
        contribute(gy, 1)
        pair.wait()
        ahead = [lax.rem(gx + d, nx) for d in range(nx)]
        for x in ahead[1:]:
            send_ref[slot, gy, x] = send_ref[slot, gy, x] + pair_ref[slot, x]
            line_copy(x, gx).start()
        line_ref[slot, gx] = send_ref[slot, gy, gx] + pair_ref[slot, gx]

        @pl.when(k + 1 < blocks)
        def _():
            pick(k + 1)

        @pl.when(k + 1 == blocks)
        def _():
            base_ref[...] = flat_ref[...]
            for q in range(quarters):
                part_ref[:, 2 * q * PAD:2 * (q + 1) * PAD] = split_ref[q]

        @pl.when(k == 1)
        def _():
            change_ref[...] = mixing_ref[...]

        @pl.when(k > 1)
        def _():
            mixing, change = mixing_ref[...], change_ref[...]
            change_ref[...] = change + mixing + apply(mixing, stack(*split(change)))

        @pl.when(k > 0)
        def _():
            stacked = stack(part_ref[0:members, :], part_ref[members:2 * members, :])
            base = base_ref[...] + apply(change_ref[...], stacked)
            base_ref[...] = base
            high, low = split(base)
            part_ref[0:members, :] = high
            part_ref[members:2 * members, :] = low

        next_ref[...] = stack(part_ref[0:members, :], part_ref[members:2 * members, :])

        for x in ahead[1:]:
            line_copy(x, gx).wait_send()
            line_copy(x, x).wait_recv()
        top = line_ref[slot, 0]
        for x in range(1, nx):
            top = top + line_ref[slot, x]
        turned = jnp.concatenate([top, jnp.zeros((PAD - mid, PAD), F32)], axis=0).T
        bottom = jnp.where(top_lane < mid, turned[mid:members], pltpu.roll(top, PAD - mid, 1))
        last = members + mid
        shift = turned[last + 1:last + 2] + pltpu.roll(turned[last:last + 8], mid, 1)[0:1]
        mixing = shift - jnp.concatenate([top, bottom], axis=0)
        mixing = jnp.where(lane < members, mixing, 0.0)
        centre = jnp.sum(mixing, axis=1, keepdims=True) / members
        mixing = jnp.where(lane < members, mixing - centre, 0.0)
        mixing_ref[...] = mixing

        @pl.when(k + 1 < blocks)
        def _():
            prior_ref[...] = base_ref[...] + apply(mixing, next_ref[...])

        return carry

    lax.fori_loop(0, blocks, assimilate, 0)
    base, mixing = own_rows(base_ref[...]), mixing_ref[...]
    mine = base + apply(own_rows(mixing), next_ref[...])
    for lev in range(levels):
        for x in range(cx):
            s = lev * cx + x
            out_ref[:, lev, x, :] = mine[0:members_dev, s * cy:(s + 1) * cy]


def local(
    ensemble, wind_field, obs_value, obs_var, obs_region, obs_cell, block_order, localization
):
    nx, ny, nm = lax.axis_size("gx"), lax.axis_size("gy"), lax.axis_size("ma")
    members_dev, levels, cx, cy = ensemble.shape
    half = members_dev // 2
    members = members_dev * nm
    blocks, obs = obs_value.shape
    rows = levels * cx
    cells = rows * cy
    regions = nx * ny
    width = 4 if nx % 4 == 0 else nx
    dma = pltpu.SemaphoreType.DMA
    vmem = pl.BlockSpec(memory_space=pltpu.VMEM)
    return pl.pallas_call(
        functools.partial(kernel, nx, ny, nm),
        out_shape=jax.ShapeDtypeStruct(ensemble.shape, F32),
        in_specs=[pl.BlockSpec(memory_space=pltpu.SMEM)] + [pl.BlockSpec(memory_space=pl.ANY)] * 7,
        out_specs=vmem,
        scratch_shapes=[
            pltpu.VMEM(ensemble.shape, F32),
            pltpu.VMEM(wind_field.shape, F32),
            pltpu.VMEM(obs_value.shape, F32),
            pltpu.VMEM(obs_var.shape, F32),
            pltpu.VMEM(obs_region.shape, jnp.int32),
            pltpu.VMEM(obs_cell.shape, jnp.int32),
            pltpu.VMEM(localization.shape, F32),
            dma((7,)),
            pltpu.VMEM((half, levels, cx, cy), F32),
            pltpu.VMEM(wind_field.shape, F32),
            pltpu.VMEM((ny, half + 2, 2 * levels, cy), F32),
            pltpu.VMEM((ny, half + 2, 2 * levels, cy), F32),
            pltpu.VMEM((ny, half + 2, 2 * levels, cy), F32),
            pltpu.VMEM((ny, half + 2, 2 * levels, cy), F32),
            pltpu.VMEM((half + 2, levels, cx + 4, 2 * cy), F32),
            pltpu.VMEM((ny, half, rows, cy), F32),
            pltpu.VMEM((members, rows, cy), F32),
            pltpu.VMEM((members, cells), F32),
            pltpu.VMEM((cells // (2 * PAD), 2 * members, 2 * PAD), BF),
            pltpu.VMEM((regions, blocks, obs), F32),
            pltpu.VMEM((blocks, 2 * PAD, obs), BF),
            pltpu.VMEM((blocks, 1, obs), jnp.int32),
            pltpu.VMEM((2, 2 * width * members, obs), BF),
            pltpu.VMEM((3 * members, cells), BF),
            pltpu.VMEM((2 * PAD, obs), BF),
            pltpu.VMEM((obs, 2 * PAD), BF),
            pltpu.VMEM((2, ny, nx, members // 2, PAD), F32),
            pltpu.VMEM((2, nx, members // 2, PAD), F32),
            pltpu.VMEM((2, nx, members // 2, PAD), F32),
            pltpu.VMEM((members, obs), F32),
            pltpu.VMEM((2 * members, obs), BF),
            pltpu.VMEM((members, obs), F32),
            pltpu.VMEM((members, PAD), F32),
            pltpu.VMEM((members, PAD), F32),
            dma((4,)),
            dma((2, ny)),
            dma((2, ny)),
            dma((regions,)),
            dma((regions,)),
            dma((nm * ny,)),
            dma((nm * ny,)),
            dma((2, 2)),
            dma((2, nx)),
            dma((2, nx)),
        ],
        compiler_params=pltpu.CompilerParams(
            collective_id=0, has_side_effects=True, vmem_limit_bytes=56 * 1024 * 1024
        ),
    )(block_order, ensemble, wind_field, obs_value, obs_var, obs_region, obs_cell, localization)


def solution(mesh):
    in_specs = (
        P("ma", None, "gx", "gy"),
        P(None, None, "gx", "gy"),
        P(),
        P(),
        P(),
        P(),
        P(),
        P("gx", "gy", None, None),
    )
    out_specs = P("ma", None, "gx", "gy")
    return jax.shard_map(local, mesh=mesh, in_specs=in_specs, out_specs=out_specs, check_vma=False)
```
